512 devices in a mesh: space: 128 (over z, y, core), snap: 4 (over x).
Axes of the slice: x: 4, y: 8, z: 8, core: 2. Of those that a mesh axis runs over, the one named last changes fastest.
Arguments:
- direct_snaps: bfloat16 [256, 3, 512, 8, 128], P('snap', None, 'space'), may hold values from -24 to 24
- adjoint_snaps: bfloat16 [256, 3, 512, 8, 128], P('snap', None, 'space'), may hold values from -6 to 6
- left_factor: float32 [256, 64], replicated, may hold values from -0.375 to 0.375
- right_factor: float32 [256, 64], replicated, may hold values from -0.375 to 0.375
- singular: float32 [64], replicated, may hold values from 1 to 100
- term_coeff: float32 [16, 512, 8, 128], P(None, 'space'), may hold values from -6 to 6
- term_slot: int32 [16], replicated, may hold values from 0 to 15, each once
Outputs:
- cross_gram: float32 [256, 256], P('snap', 'space')
- reduced_ops: float32 [1024, 64], P('space', 'snap')
The draws below stay inside these ranges and needn't reach their ends.
Inputs may be any that keep to these rules, and one draw needn't show every extreme that they name: term_slot is a permutation: each of the 16 slots holds the operator of exactly one term.
All inputs are finite; a program needn't handle non-finite values.
Results may differ from the reference program's by a relative error of at most 0.00105.
The reference program's roundings to bfloat16 on the way (of `direct_weight`, `adjoint_weight`, `direct_modes` and `weighted`) count: a program that leaves them out, or rounds other values in their place, can miss the bound.
Values may be sent and summed in bfloat16 or wider, within the bound.
No kernel may reach another device: no remote copies, remote signals or barrier semaphores. Data moves between devices by JAX's collectives and lax.ppermute only.
A program may use at most 128 MiB of HBM per device.

```python
import math
import jax
import jax.numpy as jnp
from jax import lax

M = 256
R = 64
Q = 16
COMPONENTS = 3
NY = 8
NZ = 128
NX = 512
NSTATE = 1572864


def raised(result, key, source, target, parts, factor):
    def block_of(position):
        return (jnp.arange(result.shape[position]) // (result.shape[position] // parts)).reshape((-1,) + (1,) * (result.ndim - 1 - position))

    near = jax.random.permutation(key, parts)[block_of(target)]
    far = (block_of(target) + parts // 2) % parts
    return jnp.where((block_of(source) == near) | (block_of(source) == far), factor * result, result)


def levels(stream_key, dims, shards, smallest, top_value):
    gain = 1.0
    for axis_at, blocks in shards:
        steps = jax.random.uniform(jax.random.fold_in(jax.random.fold_in(stream_key, 6), axis_at), (blocks,), jnp.float32, smallest / len(shards), top_value / len(shards))
        gain = gain * jnp.repeat(jnp.exp(steps), dims[axis_at] // blocks).reshape((-1,) + (1,) * (len(dims) - 1 - axis_at))
    return gain


def bell_draw(rng, extent, width, limit, shards=(), dtype=jnp.bfloat16):
    gain = levels(rng, extent, shards, -0.22, 0.18) if shards else 1.0
    values = jax.random.normal(rng, extent, jnp.float32) * width * gain
    return jnp.minimum(jnp.maximum(values, -limit), limit).astype(dtype)


def heavy_noise(stream_key, extent, scale, most, cuts, heavy, kind=jnp.bfloat16):
    values = scale * jax.random.normal(stream_key, extent, jnp.float32)
    if cuts:
        values = values * levels(stream_key, extent, cuts, -0.22, 0.18)
    return jnp.clip(raised(values, jax.random.fold_in(stream_key, 3), *heavy), -most, most).astype(kind)


def setup_inputs(seed: int = 0) -> dict:
    streams_of = jax.random.split(jax.random.key(seed), 8)
    return {
        "direct_snaps": heavy_noise(streams_of[0], (M, COMPONENTS, NX, NY, NZ), 1.0, 24.0, ((0, 4), (2, 128)), (2, 0, 128, 5.5)),
        "adjoint_snaps": bell_draw(streams_of[1], (M, COMPONENTS, NX, NY, NZ), 1.0, 6.0, ((0, 4), (2, 128))),
        "left_factor": bell_draw(streams_of[2], (M, R), M ** -0.5, 0.375, (), jnp.float32),
        "right_factor": bell_draw(streams_of[3], (M, R), M ** -0.5, 0.375, (), jnp.float32),
        "singular": jnp.clip(jnp.exp(jax.random.uniform(streams_of[4], (R,), jnp.float32, math.log(1.0), math.log(100.0))), 1.0, 100.0),
        "term_coeff": bell_draw(streams_of[5], (Q, NX, NY, NZ), 1.0, 6.0, ((1, 128),), jnp.float32),
        "term_slot": jax.random.permutation(streams_of[6], Q).astype(jnp.int32),
    }


stencil_kind = (4, 4, 4, 1, 2, 3, 1, 2, 3, 1, 2, 3, 0, 0, 0, 0)
source_comp = (0, 1, 2, 0, 0, 0, 1, 1, 1, 2, 2, 2, 0, 1, 2, 1)
target_comp = (0, 1, 2, 0, 0, 0, 1, 1, 1, 2, 2, 2, 1, 2, 0, 0)

def apply_stencil(padded, kind):
    center = padded[..., 1:-1, 1:-1, 1:-1]
    if kind == 0:
        return center
    if kind == 1:
        return 0.5 * (padded[..., 2:, 1:-1, 1:-1] - padded[..., :-2, 1:-1, 1:-1])
    if kind == 2:
        return 0.5 * (padded[..., 1:-1, 2:, 1:-1] - padded[..., 1:-1, :-2, 1:-1])
    if kind == 3:
        return 0.5 * (padded[..., 1:-1, 1:-1, 2:] - padded[..., 1:-1, 1:-1, :-2])
    beside_all = padded[..., 2:, 1:-1, 1:-1] + padded[..., :-2, 1:-1, 1:-1]
    beside_all = beside_all + padded[..., 1:-1, 2:, 1:-1] + padded[..., 1:-1, :-2, 1:-1]
    beside_all = beside_all + padded[..., 1:-1, 1:-1, 2:] + padded[..., 1:-1, 1:-1, :-2]
    return beside_all - 6.0 * center

def mode_weight(factor, singular):
    return (factor / jnp.sqrt(singular)[None, :]).astype(jnp.bfloat16)

def reference(direct_snaps, adjoint_snaps, left_factor, right_factor, singular, term_coeff, term_slot):
    norm_scale = 1.0 / math.sqrt(NSTATE)
    contract_state = (((1,), (1,)), ((), ()))
    contract_lead = (((0,), (0,)), ((), ()))
    flat_direct = direct_snaps.reshape(M, NSTATE)
    flat_adjoint = adjoint_snaps.reshape(M, NSTATE)
    cross_gram = lax.dot_general(flat_adjoint, flat_direct, contract_state, preferred_element_type=jnp.float32) * norm_scale
    direct_weight = mode_weight(right_factor, singular)
    adjoint_weight = mode_weight(left_factor, singular)
    direct_modes = lax.dot_general(direct_weight, flat_direct, contract_lead, preferred_element_type=jnp.float32).astype(jnp.bfloat16)
    adjoint_modes = lax.dot_general(adjoint_weight, flat_adjoint, contract_lead, preferred_element_type=jnp.float32)
    direct_modes = direct_modes.reshape(R, COMPONENTS, NX, NY, NZ)
    adjoint_modes = adjoint_modes.reshape(R, COMPONENTS, NX * NY * NZ)
    operators = []
    for term_index in range(Q):
        field = direct_modes[:, source_comp[term_index]]
        padded = jnp.pad(field, ((0, 0), (1, 1), (1, 1), (1, 1))).astype(jnp.float32)
        shaped = apply_stencil(padded, stencil_kind[term_index]) * term_coeff[term_index][None]
        weighted = shaped.astype(jnp.bfloat16).reshape(R, NX * NY * NZ).astype(jnp.float32)
        product = lax.dot_general(adjoint_modes[:, target_comp[term_index]], weighted, contract_state, precision=lax.Precision.HIGHEST, preferred_element_type=jnp.float32)
        operators.append(product * norm_scale)
    stacked = jnp.stack(operators)
    ordered = jnp.zeros_like(stacked).at[term_slot].set(stacked)
    return (cross_gram, ordered.reshape(Q * R, R))
```

```python
import functools
import math

import jax
import jax.numpy as jnp
from jax import lax
from jax.experimental import pallas as pl
from jax.experimental.pallas import tpu as pltpu
from jax.sharding import Mesh, PartitionSpec as P

stencil_kind = (4, 4, 4, 1, 2, 3, 1, 2, 3, 1, 2, 3, 0, 0, 0, 0)
source_comp = (0, 1, 2, 0, 0, 0, 1, 1, 1, 2, 2, 2, 0, 1, 2, 1)
target_comp = (0, 1, 2, 0, 0, 0, 1, 1, 1, 2, 2, 2, 1, 2, 0, 0)
TERMS = len(stencil_kind)
COMPONENTS = 3
MEMBERS = tuple(
    tuple(q for q in range(TERMS) if target_comp[q] == target) for target in range(COMPONENTS)
)
ORDER = tuple(q for members in MEMBERS for q in members)
M = 256
R = 64
NY = 8
NZ = 128
CELLS = NY * NZ
SNAP = 4
COLS = M // SNAP
OWN = R // SNAP
SPACE = ("z", "y", "core")
CHUNKS = 8
LIMIT = 50 * 1024 * 1024


def mode_weight(factor, singular):
    return (factor / jnp.sqrt(singular)[None, :]).astype(jnp.bfloat16)


def columns(ref, comp, rows):
    return jnp.concatenate(
        [jnp.concatenate([ref[s, comp, y] for s in range(SNAP)], axis=0) for y in rows], axis=1
    )


def modes_kernel(snaps_ref, weight_ref, out_ref):
    weight = weight_ref[...]
    for comp in range(COMPONENTS):
        for y in range(0, NY, 2):
            block = columns(snaps_ref, comp, (y, y + 1))
            modes = jnp.dot(weight, block, preferred_element_type=jnp.float32)
            modes = modes.astype(jnp.bfloat16)
            out_ref[comp, y] = modes[:, :NZ]
            out_ref[comp, y + 1] = modes[:, NZ:]


def weighted_kernel(modes_ref, before_ref, after_ref, coeff_ref, out_ref):
    lane = lax.broadcasted_iota(jnp.int32, (R, NZ), 1)
    zero = jnp.zeros((R, NZ), jnp.float32)
    base = [0]
    for members in MEMBERS:
        base.append(base[-1] + len(members) * R)

    def put(q, y, value):
        target = target_comp[q]
        count = len(MEMBERS[target])
        at = MEMBERS[target].index(q)
        value = (value * coeff_ref[q, y : y + 1, :]).astype(jnp.bfloat16)
        for block in range(SNAP):
            row = base[target] + (block * count + at) * OWN
            out_ref[row : row + OWN, y * NZ : (y + 1) * NZ] = value[block * OWN : (block + 1) * OWN]

    for comp in range(COMPONENTS):
        field = [modes_ref[comp, y].astype(jnp.float32) for y in range(NY)]
        for y in range(NY):
            center = field[y]
            x_up = after_ref[comp, y].astype(jnp.float32)
            x_down = before_ref[comp, y].astype(jnp.float32)
            y_up = field[y + 1] if y + 1 < NY else zero
            y_down = field[y - 1] if y > 0 else zero
            z_up = jnp.where(lane == NZ - 1, 0.0, pltpu.roll(center, NZ - 1, 1))
            z_down = jnp.where(lane == 0, 0.0, pltpu.roll(center, 1, 1))
            for q in range(TERMS):
                if source_comp[q] != comp:
                    continue
                kind = stencil_kind[q]
                if kind == 0:
                    value = center
                elif kind == 1:
                    value = 0.5 * (x_up - x_down)
                elif kind == 2:
                    value = 0.5 * (y_up - y_down)
                elif kind == 3:
                    value = 0.5 * (z_up - z_down)
                else:
                    beside = x_up + x_down
                    beside = beside + y_up + y_down
                    beside = beside + z_up + z_down
                    value = beside - 6.0 * center
                put(q, y, value)


def products_kernel(scale, adjoint_ref, direct_ref, weight_ref, weighted_ref, out_ref, gram_ref, parts_ref):
    transposed = (((1,), (1,)), ((), ()))
    weight = weight_ref[...]
    gram = jnp.zeros((M, M), jnp.float32)
    for comp in range(COMPONENTS):
        for y in range(0, NY, 2):
            adjoint = columns(adjoint_ref, comp, (y, y + 1))
            direct = columns(direct_ref, comp, (y, y + 1))
            gram = gram + lax.dot_general(
                direct, adjoint, transposed, preferred_element_type=jnp.float32
            )
            modes = jnp.dot(weight, adjoint, preferred_element_type=jnp.float32)
            high = modes.astype(jnp.bfloat16)
            rest = modes - high.astype(jnp.float32)
            middle = rest.astype(jnp.bfloat16)
            low = (rest - middle.astype(jnp.float32)).astype(jnp.bfloat16)
            for part, value in enumerate((high, middle, low)):
                parts_ref[comp, part * R : (part + 1) * R, y * NZ : (y + 2) * NZ] = value
    gram = gram * scale
    gram_ref[0] = gram[:, :NZ]
    gram_ref[1] = gram[:, NZ:]
    for core in range(2):
        for snap in range(SNAP):
            half, at = snap // 2, (snap % 2) * COLS
            halves = [
                gram_ref[half, pl.ds(2 * core + t, M // 4, stride=4), :][:, at : at + COLS]
                for t in range(2)
            ]
            out_ref[core * SNAP + snap, :64, :] = jnp.concatenate(halves, axis=1)
    blocks = []
    row = 0
    for target, members in enumerate(MEMBERS):
        count = len(members) * R
        product = lax.dot_general(
            parts_ref[target],
            weighted_ref[row : row + count, :],
            transposed,
            preferred_element_type=jnp.float32,
        )
        row += count
        blocks.append((product[:R] + (product[R : 2 * R] + product[2 * R :])) * scale)
    for snap in range(SNAP):
        own = jnp.concatenate(
            [
                block[:, snap * (block.shape[1] // SNAP) : (snap + 1) * (block.shape[1] // SNAP)]
                for block in blocks
            ],
            axis=1,
        )
        for core in range(2):
            for w in range(4):
                rows = own[(2 * w + core) * 8 : (2 * w + core + 1) * 8]
                out_ref[core * SNAP + snap, 64 + w * 8 : 64 + w * 8 + 8, :] = rows[:, :NZ]
                out_ref[core * SNAP + snap, 96 + w * 8 : 96 + w * 8 + 8, :] = rows[:, NZ:]


def call(kernel, out_shape, flops, moved, scratch=()):
    return pl.pallas_call(
        kernel,
        out_shape=out_shape,
        scratch_shapes=list(scratch),
        compiler_params=pltpu.CompilerParams(vmem_limit_bytes=LIMIT),
        cost_estimate=pl.CostEstimate(flops=flops, bytes_accessed=moved, transcendentals=0),
    )


def shards(direct_snaps, adjoint_snaps, left_factor, right_factor, singular, term_coeff, term_slot):
    scale = 1.0 / math.sqrt(1572864)
    snap = lax.axis_index("snap")
    direct_weight = mode_weight(right_factor, singular).T
    adjoint_weight = mode_weight(left_factor, singular).T
    coeff = lax.dynamic_index_in_dim(term_coeff, snap, 1, keepdims=False)

    def spread(snaps):
        layers = snaps.transpose(2, 1, 3, 0, 4)
        return lax.all_to_all(layers, "snap", 0, 0, tiled=True)

    direct = spread(direct_snaps)
    adjoint = spread(adjoint_snaps)
    mode_shape = jax.ShapeDtypeStruct((COMPONENTS, NY, R, NZ), jnp.bfloat16)
    modes = call(modes_kernel, mode_shape, 2 * R * M * 3 * CELLS, 2 << 20)(direct, direct_weight)
    flat = SPACE + ("snap",)
    up = [(i, i + 1) for i in range(511)]
    before = lax.ppermute(modes, flat, up)
    after = lax.ppermute(modes, flat, [(j, i) for i, j in up])
    weighted = call(
        weighted_kernel, jax.ShapeDtypeStruct((TERMS * R, CELLS), jnp.bfloat16), 1 << 26, 3 << 20
    )(modes, before, after, coeff)
    terms = call(
        functools.partial(products_kernel, scale),
        jax.ShapeDtypeStruct((CHUNKS, 128, NZ), jnp.float32),
        1 << 30,
        6 << 20,
        (
            pltpu.VMEM((2, M, NZ), jnp.float32),
            pltpu.VMEM((COMPONENTS, 3 * R, CELLS), jnp.bfloat16),
        ),
    )(adjoint, direct, adjoint_weight, weighted)
    near = lax.all_to_all(terms, ("core", "snap"), 0, 0, tiled=True).sum(axis=0)
    gram = near[:64]
    operators = near[64:].reshape(2, 4, 8, 8, OWN).transpose(0, 3, 1, 2, 4).reshape(TERMS, 4 * NZ)
    selector = (
        term_slot[jnp.array(ORDER)][None, :] == jnp.arange(TERMS, dtype=jnp.int32)[:, None]
    ).astype(jnp.float32)
    ordered = jnp.dot(selector, operators, precision=lax.Precision.HIGHEST)
    owned = jnp.stack([gram, ordered.reshape(64, NZ)], axis=1)
    final = lax.all_to_all(owned, ("z", "y"), 0, 0, tiled=True).sum(axis=0)
    return (final[0].reshape(2, COLS).T, final[1].reshape(8, OWN))


def solution(mesh):
    parts = Mesh(mesh.devices.reshape(8, 8, 2, 4), SPACE + ("snap",))
    return jax.shard_map(
        shards,
        mesh=parts,
        in_specs=(
            P("snap", None, SPACE, None, None),
            P("snap", None, SPACE, None, None),
            P(),
            P(),
            P(),
            P(None, SPACE, None, None),
            P(),
        ),
        out_specs=(P("snap", SPACE), P(SPACE, "snap")),
        check_vma=False,
    )
```

```python
import functools
import math

import jax
import jax.numpy as jnp
from jax import lax
from jax.experimental import pallas as pl
from jax.experimental.pallas import tpu as pltpu
from jax.sharding import Mesh, PartitionSpec as P

stencil_kind = (4, 4, 4, 1, 2, 3, 1, 2, 3, 1, 2, 3, 0, 0, 0, 0)
source_comp = (0, 1, 2, 0, 0, 0, 1, 1, 1, 2, 2, 2, 0, 1, 2, 1)
target_comp = (0, 1, 2, 0, 0, 0, 1, 1, 1, 2, 2, 2, 1, 2, 0, 0)
TERMS = len(stencil_kind)
COMPONENTS = 3
MEMBERS = tuple(
    tuple(q for q in range(TERMS) if target_comp[q] == target) for target in range(COMPONENTS)
)
ORDER = tuple(q for members in MEMBERS for q in members)
M = 256
R = 64
NY = 8
NZ = 128
CELLS = NY * NZ
SNAP = 4
COLS = M // SNAP
OWN = R // SNAP
SPACE = ("z", "y", "core")
CHUNKS = 8
LIMIT = 24 * 1024 * 1024


def mode_weight(factor, singular):
    return (factor / jnp.sqrt(singular)[None, :]).astype(jnp.bfloat16)


TILES = 8
GROUP = NZ // SNAP


def spread_tiles(snaps_ref, out_ref):
    for comp in range(COMPONENTS):
        for x in range(4):
            rows = jnp.swapaxes(snaps_ref[:, comp, x], 0, 1)
            for half in range(2):
                group = [rows[half * 4 + i] for i in range(4)]
                for quarter in range(SNAP):
                    at = quarter * GROUP
                    out_ref[quarter, comp * TILES + x * 2 + half] = jnp.concatenate(
                        [row[:, at : at + GROUP] for row in group], axis=1
                    )


def direct_kernel(snaps_ref, out_ref):
    spread_tiles(snaps_ref, out_ref)


def adjoint_kernel(
    snap_ref, snaps_ref, left_ref, right_ref, coeff_ref, out_ref, left_out, right_out, coeff_out
):
    spread_tiles(snaps_ref, out_ref)
    left_out[...] = left_ref[...]
    right_out[...] = right_ref[...]
    shift = lax.rem(NZ - GROUP * snap_ref[0], NZ)
    for q in range(TERMS):
        for x in range(4):
            own = pltpu.roll(coeff_ref[q, x], shift, 1)
            for half in range(2):
                coeff_out[q, x * 2 + half : x * 2 + half + 1, :] = jnp.concatenate(
                    [own[half * 4 + i : half * 4 + i + 1, :GROUP] for i in range(4)], axis=1
                )


def columns(ref, comp, tiles):
    return jnp.concatenate(
        [
            jnp.concatenate([ref[s, comp * TILES + t] for s in range(SNAP)], axis=0)
            for t in tiles
        ],
        axis=1,
    )


def modes_kernel(snaps_ref, weight_ref, out_ref, first_ref, last_ref, low_ref, high_ref):
    weight = weight_ref[...]
    place = lax.rem(lax.broadcasted_iota(jnp.int32, (R, NZ), 1), GROUP)
    low = jnp.zeros((R, NZ), jnp.float32)
    high = jnp.zeros((R, NZ), jnp.float32)
    for comp in range(COMPONENTS):
        for t in range(0, TILES, 2):
            block = columns(snaps_ref, comp, (t, t + 1))
            modes = jnp.dot(weight, block, preferred_element_type=jnp.float32)
            modes = modes.astype(jnp.bfloat16)
            for half in range(2):
                tile = modes[:, half * NZ : (half + 1) * NZ]
                index = comp * TILES + t + half
                out_ref[index] = tile
                if t == 0:
                    first_ref[comp * 2 + half] = tile
                if t == TILES - 2:
                    last_ref[comp * 2 + half] = tile
                wide = tile.astype(jnp.float32)
                edge = jnp.where(place == 0, wide, 0.0)
                low = low + (pltpu.roll(edge, index, 1) if index else edge)
                edge = jnp.where(place == GROUP - 1, wide, 0.0)
                high = high + pltpu.roll(edge, NZ + index - (GROUP - 1), 1)
    low_ref[...] = low.astype(jnp.bfloat16)
    high_ref[...] = high.astype(jnp.bfloat16)


def weighted_kernel(
    modes_ref, before_ref, after_ref, below_ref, above_ref, coeff_ref, out_ref
):
    lane = lax.broadcasted_iota(jnp.int32, (R, NZ), 1)
    place = lax.rem(lane, GROUP)
    below = below_ref[...].astype(jnp.float32)
    above = above_ref[...].astype(jnp.float32)
    base = [0]
    for members in MEMBERS:
        base.append(base[-1] + len(members) * R)

    def put(q, t, value):
        target = target_comp[q]
        count = len(MEMBERS[target])
        at = MEMBERS[target].index(q)
        value = (value * coeff_ref[q, t : t + 1, :]).astype(jnp.bfloat16)
        for block in range(SNAP):
            row = base[target] + (block * count + at) * OWN
            out_ref[row : row + OWN, t * NZ : (t + 1) * NZ] = value[block * OWN : (block + 1) * OWN]

    for comp in range(COMPONENTS):
        field = [modes_ref[comp * TILES + t].astype(jnp.float32) for t in range(TILES)]
        down = [before_ref[comp * 2 + h].astype(jnp.float32) for h in range(2)] + field[:-2]
        up = field[2:] + [after_ref[comp * 2 + h].astype(jnp.float32) for h in range(2)]
        for x in range(4):
            pair = field[2 * x : 2 * x + 2]
            ahead = [pltpu.roll(v, NZ - GROUP, 1) for v in pair]
            behind = [pltpu.roll(v, GROUP, 1) for v in pair]
            for half in range(2):
                t = 2 * x + half
                index = comp * TILES + t
                center = pair[half]
                x_up, x_down = up[t], down[t]
                y_up = jnp.where(lane >= NZ - GROUP, ahead[1] if half == 0 else 0.0, ahead[half])
                y_down = jnp.where(lane < GROUP, behind[0] if half == 1 else 0.0, behind[half])
                z_up = jnp.where(
                    place == GROUP - 1,
                    pltpu.roll(above, GROUP - 1 - index, 1),
                    pltpu.roll(center, NZ - 1, 1),
                )
                z_down = jnp.where(
                    place == 0,
                    pltpu.roll(below, NZ - index, 1) if index else below,
                    pltpu.roll(center, 1, 1),
                )
                for q in range(TERMS):
                    if source_comp[q] != comp:
                        continue
                    kind = stencil_kind[q]
                    if kind == 0:
                        value = center
                    elif kind == 1:
                        value = 0.5 * (x_up - x_down)
                    elif kind == 2:
                        value = 0.5 * (y_up - y_down)
                    elif kind == 3:
                        value = 0.5 * (z_up - z_down)
                    else:
                        beside = x_up + x_down
                        beside = beside + y_up + y_down
                        beside = beside + z_up + z_down
                        value = beside - 6.0 * center
                    put(q, t, value)


def products_kernel(scale, adjoint_ref, direct_ref, weight_ref, weighted_ref, out_ref, gram_ref, parts_ref):
    transposed = (((1,), (1,)), ((), ()))
    weight = weight_ref[...]
    gram = jnp.zeros((M, M), jnp.float32)
    for comp in range(COMPONENTS):
        for t in range(0, TILES, 2):
            adjoint = columns(adjoint_ref, comp, (t, t + 1))
            direct = columns(direct_ref, comp, (t, t + 1))
            gram = gram + lax.dot_general(
                direct, adjoint, transposed, preferred_element_type=jnp.float32
            )
            modes = jnp.dot(weight, adjoint, preferred_element_type=jnp.float32)
            high = modes.astype(jnp.bfloat16)
            rest = modes - high.astype(jnp.float32)
            middle = rest.astype(jnp.bfloat16)
            low = (rest - middle.astype(jnp.float32)).astype(jnp.bfloat16)
            for part, value in enumerate((high, middle, low)):
                parts_ref[comp, part * R : (part + 1) * R, t * NZ : (t + 2) * NZ] = value
    gram = gram * scale
    gram_ref[0] = gram[:, :NZ]
    gram_ref[1] = gram[:, NZ:]
    for core in range(2):
        for snap in range(SNAP):
            half, at = snap // 2, (snap % 2) * COLS
            halves = [
                gram_ref[half, pl.ds(2 * core + t, M // 4, stride=4), :][:, at : at + COLS]
                for t in range(2)
            ]
            out_ref[core * SNAP + snap, :64, :] = jnp.concatenate(halves, axis=1)
    blocks = []
    row = 0
    for target, members in enumerate(MEMBERS):
        count = len(members) * R
        product = lax.dot_general(
            parts_ref[target],
            weighted_ref[row : row + count, :],
            transposed,
            preferred_element_type=jnp.float32,
        )
        row += count
        blocks.append((product[:R] + (product[R : 2 * R] + product[2 * R :])) * scale)
    for snap in range(SNAP):
        own = jnp.concatenate(
            [
                block[:, snap * (block.shape[1] // SNAP) : (snap + 1) * (block.shape[1] // SNAP)]
                for block in blocks
            ],
            axis=1,
        )
        for core in range(2):
            for w in range(4):
                rows = own[(2 * w + core) * 8 : (2 * w + core + 1) * 8]
                out_ref[core * SNAP + snap, 64 + w * 8 : 64 + w * 8 + 8, :] = rows[:, :NZ]
                out_ref[core * SNAP + snap, 96 + w * 8 : 96 + w * 8 + 8, :] = rows[:, NZ:]


def call(kernel, out_shape, flops, moved, scratch=(), smem=0):
    def run(*operands):
        spaces = [pltpu.SMEM] * smem + [pltpu.VMEM] * (len(operands) - smem)
        return pl.pallas_call(
            kernel,
            out_shape=out_shape,
            in_specs=[pl.BlockSpec(memory_space=space) for space in spaces],
            scratch_shapes=list(scratch),
            compiler_params=pltpu.CompilerParams(vmem_limit_bytes=LIMIT),
            cost_estimate=pl.CostEstimate(flops=flops, bytes_accessed=moved, transcendentals=0),
        )(*operands)

    return run


def shards(direct_snaps, adjoint_snaps, left_factor, right_factor, singular, term_coeff, term_slot):
    scale = 1.0 / math.sqrt(1572864)
    left = mode_weight(left_factor, singular).T
    right = mode_weight(right_factor, singular).T
    tiles = COMPONENTS * TILES

    def shape(*dims, dtype=jnp.bfloat16):
        return jax.ShapeDtypeStruct(dims, dtype)

    spread_shape = shape(SNAP, tiles, COLS, NZ)
    ready = call(direct_kernel, spread_shape, 0, 3 << 20)(direct_snaps)
    direct = lax.all_to_all(ready, "snap", 0, 0, tiled=True)
    here = lax.axis_index("snap").astype(jnp.int32).reshape(1)
    ready, adjoint_weight, direct_weight, coeff = call(
        adjoint_kernel,
        (
            spread_shape,
            shape(R, M),
            shape(R, M),
            shape(TERMS, TILES, NZ, dtype=jnp.float32),
        ),
        0,
        3 << 20,
        smem=1,
    )(here, adjoint_snaps, left, right, term_coeff)
    adjoint = lax.all_to_all(ready, "snap", 0, 0, tiled=True)
    modes, first, last, low, high = call(
        modes_kernel,
        (shape(tiles, R, NZ), shape(6, R, NZ), shape(6, R, NZ), shape(R, NZ), shape(R, NZ)),
        2 * R * M * 3 * CELLS,
        2 << 20,
    )(direct, direct_weight)
    slabs, quarters = ([(i, i + 1) for i in range(n - 1)] for n in (128, SNAP))
    before = lax.ppermute(last, SPACE, slabs)
    after = lax.ppermute(first, SPACE, [(j, i) for i, j in slabs])
    below = lax.ppermute(high, "snap", quarters)
    above = lax.ppermute(low, "snap", [(j, i) for i, j in quarters])
    weighted = call(weighted_kernel, shape(TERMS * R, CELLS), 1 << 26, 3 << 20)(
        modes, before, after, below, above, coeff
    )
    terms = call(
        functools.partial(products_kernel, scale),
        jax.ShapeDtypeStruct((CHUNKS, 128, NZ), jnp.float32),
        1 << 30,
        6 << 20,
        (
            pltpu.VMEM((2, M, NZ), jnp.float32),
            pltpu.VMEM((COMPONENTS, 3 * R, CELLS), jnp.bfloat16),
        ),
    )(adjoint, direct, adjoint_weight, weighted)
    near = lax.all_to_all(terms, ("core", "snap"), 0, 0, tiled=True).sum(axis=0)
    gram = near[:64]
    operators = near[64:].reshape(2, 4, 8, 8, OWN).transpose(0, 3, 1, 2, 4).reshape(TERMS, 4 * NZ)
    selector = (
        term_slot[jnp.array(ORDER)][None, :] == jnp.arange(TERMS, dtype=jnp.int32)[:, None]
    ).astype(jnp.float32)
    ordered = jnp.dot(selector, operators, precision=lax.Precision.HIGHEST)
    owned = jnp.stack([gram, ordered.reshape(64, NZ)], axis=1)
    final = lax.all_to_all(owned, ("z", "y"), 0, 0, tiled=True).sum(axis=0)
    return (final[0].reshape(2, COLS).T, final[1].reshape(8, OWN))


def solution(mesh):
    parts = Mesh(mesh.devices.reshape(8, 8, 2, 4), SPACE + ("snap",))
    return jax.shard_map(
        shards,
        mesh=parts,
        in_specs=(
            P("snap", None, SPACE, None, None),
            P("snap", None, SPACE, None, None),
            P(),
            P(),
            P(),
            P(None, SPACE, None, None),
            P(),
        ),
        out_specs=(P("snap", SPACE), P(SPACE, "snap")),
        check_vma=False,
    )
```

```python
import functools
import math

import jax
import jax.numpy as jnp
from jax import lax
from jax.experimental import pallas as pl
from jax.experimental.pallas import tpu as pltpu
from jax.sharding import Mesh, PartitionSpec as P

stencil_kind = (4, 4, 4, 1, 2, 3, 1, 2, 3, 1, 2, 3, 0, 0, 0, 0)
source_comp = (0, 1, 2, 0, 0, 0, 1, 1, 1, 2, 2, 2, 0, 1, 2, 1)
target_comp = (0, 1, 2, 0, 0, 0, 1, 1, 1, 2, 2, 2, 1, 2, 0, 0)
TERMS = len(stencil_kind)
COMPONENTS = 3
MEMBERS = tuple(
    tuple(q for q in range(TERMS) if target_comp[q] == target) for target in range(COMPONENTS)
)
ORDER = tuple(q for members in MEMBERS for q in members)
M = 256
R = 64
NY = 8
NZ = 128
CELLS = NY * NZ
SNAP = 4
COLS = M // SNAP
OWN = R // SNAP
SPACE = ("z", "y", "core")
CHUNKS = 8
LIMIT = 24 * 1024 * 1024
WHOLE = 60 * 1024 * 1024


def mode_weight(factor, singular):
    return (factor / jnp.sqrt(singular)[None, :]).astype(jnp.bfloat16)


TILES = 8
GROUP = NZ // SNAP


def spread_rows(layer, out_ref, first):
    rows = jnp.swapaxes(layer, 0, 1)
    for half in range(2):
        group = [rows[half * 4 + i] for i in range(4)]
        for quarter in range(SNAP):
            at = quarter * GROUP
            out_ref[quarter, first + half] = jnp.concatenate(
                [row[:, at : at + GROUP] for row in group], axis=1
            )


def direct_kernel(snaps_ref, out_ref, raw, spread, arrived, sent):
    pieces = [(comp, x) for comp in range(COMPONENTS) for x in range(4)]
    arrivals = [
        pltpu.make_async_copy(snaps_ref.at[:, comp, x], raw.at[n], arrived.at[n])
        for n, (comp, x) in enumerate(pieces)
    ]
    for copy in arrivals:
        copy.start()
    departures = []
    for n, (comp, x) in enumerate(pieces):
        arrivals[n].wait()
        spread_rows(raw[n], spread, 2 * n)
        tiles = pl.ds(2 * n, 2)
        departures.append(pltpu.make_async_copy(spread.at[:, tiles], out_ref.at[:, tiles], sent.at[n]))
        departures[-1].start()
    for copy in departures:
        copy.wait()


def adjoint_kernel(
    snap_ref, snaps_ref, left_ref, right_ref, coeff_ref, out_ref, left_out, right_out, coeff_out
):
    for comp in range(COMPONENTS):
        for x in range(4):
            spread_rows(snaps_ref[:, comp, x], out_ref, comp * TILES + x * 2)
    left_out[...] = left_ref[...]
    right_out[...] = right_ref[...]
    shift = lax.rem(NZ - GROUP * snap_ref[0], NZ)
    for q in range(TERMS):
        for x in range(4):
            own = pltpu.roll(coeff_ref[q, x], shift, 1)
            for half in range(2):
                coeff_out[q, x * 2 + half : x * 2 + half + 1, :] = jnp.concatenate(
                    [own[half * 4 + i : half * 4 + i + 1, :GROUP] for i in range(4)], axis=1
                )


def columns(ref, comp, tiles):
    return jnp.concatenate(
        [
            jnp.concatenate([ref[s, comp * TILES + t] for s in range(SNAP)], axis=0)
            for t in tiles
        ],
        axis=1,
    )


def modes_kernel(
    odd_ref, snaps_ref, weight_ref, out_ref, x_near_ref, x_far_ref, z_near_ref, z_far_ref
):
    x_odd = odd_ref[0] == 1
    z_odd = odd_ref[1] == 1
    weight = weight_ref[...]
    place = lax.rem(lax.broadcasted_iota(jnp.int32, (R, NZ), 1), GROUP)
    low = jnp.zeros((R, NZ), jnp.float32)
    high = jnp.zeros((R, NZ), jnp.float32)
    first, last = [], []
    for comp in range(COMPONENTS):
        for t in range(0, TILES, 2):
            block = columns(snaps_ref, comp, (t, t + 1))
            modes = jnp.dot(weight, block, preferred_element_type=jnp.float32)
            modes = modes.astype(jnp.bfloat16)
            for half in range(2):
                tile = modes[:, half * NZ : (half + 1) * NZ]
                index = comp * TILES + t + half
                out_ref[index] = tile
                if t == 0:
                    first.append(tile)
                if t == TILES - 2:
                    last.append(tile)
                wide = tile.astype(jnp.float32)
                edge = jnp.where(place == 0, wide, 0.0)
                low = low + (pltpu.roll(edge, index, 1) if index else edge)
                edge = jnp.where(place == GROUP - 1, wide, 0.0)
                high = high + pltpu.roll(edge, NZ + index - (GROUP - 1), 1)
    z_near_ref[...] = jnp.where(z_odd, low, high).astype(jnp.bfloat16)
    z_far_ref[...] = jnp.where(z_odd, high, low).astype(jnp.bfloat16)
    for n in range(6):
        x_near_ref[n] = jnp.where(x_odd, first[n], last[n])
        x_far_ref[n] = jnp.where(x_odd, last[n], first[n])


def weighted_kernel(
    odd_ref, modes_ref, x_near_ref, x_far_ref, z_near_ref, z_far_ref, coeff_ref, out_ref
):
    lane = lax.broadcasted_iota(jnp.int32, (R, NZ), 1)
    place = lax.rem(lane, GROUP)
    x_odd = odd_ref[0] == 1
    z_odd = odd_ref[1] == 1
    z_near = z_near_ref[...].astype(jnp.float32)
    z_far = z_far_ref[...].astype(jnp.float32)
    below = jnp.where(z_odd, z_near, z_far)
    above = jnp.where(z_odd, z_far, z_near)
    x_near = [x_near_ref[n].astype(jnp.float32) for n in range(6)]
    x_far = [x_far_ref[n].astype(jnp.float32) for n in range(6)]
    before = [jnp.where(x_odd, near, far) for near, far in zip(x_near, x_far)]
    after = [jnp.where(x_odd, far, near) for near, far in zip(x_near, x_far)]
    base = [0]
    for members in MEMBERS:
        base.append(base[-1] + len(members) * R)

    def put(q, t, value):
        target = target_comp[q]
        count = len(MEMBERS[target])
        at = MEMBERS[target].index(q)
        value = (value * coeff_ref[q, t : t + 1, :]).astype(jnp.bfloat16)
        for block in range(SNAP):
            row = base[target] + (block * count + at) * OWN
            out_ref[row : row + OWN, t * NZ : (t + 1) * NZ] = value[block * OWN : (block + 1) * OWN]

    for comp in range(COMPONENTS):
        field = [modes_ref[comp * TILES + t].astype(jnp.float32) for t in range(TILES)]
        down = before[comp * 2 : comp * 2 + 2] + field[:-2]
        up = field[2:] + after[comp * 2 : comp * 2 + 2]
        for x in range(4):
            pair = field[2 * x : 2 * x + 2]
            ahead = [pltpu.roll(v, NZ - GROUP, 1) for v in pair]
            behind = [pltpu.roll(v, GROUP, 1) for v in pair]
            for half in range(2):
                t = 2 * x + half
                index = comp * TILES + t
                center = pair[half]
                x_up, x_down = up[t], down[t]
                y_up = jnp.where(lane >= NZ - GROUP, ahead[1] if half == 0 else 0.0, ahead[half])
                y_down = jnp.where(lane < GROUP, behind[0] if half == 1 else 0.0, behind[half])
                z_up = jnp.where(
                    place == GROUP - 1,
                    pltpu.roll(above, GROUP - 1 - index, 1),
                    pltpu.roll(center, NZ - 1, 1),
                )
                z_down = jnp.where(
                    place == 0,
                    pltpu.roll(below, NZ - index, 1) if index else below,
                    pltpu.roll(center, 1, 1),
                )
                for q in range(TERMS):
                    if source_comp[q] != comp:
                        continue
                    kind = stencil_kind[q]
                    if kind == 0:
                        value = center
                    elif kind == 1:
                        value = 0.5 * (x_up - x_down)
                    elif kind == 2:
                        value = 0.5 * (y_up - y_down)
                    elif kind == 3:
                        value = 0.5 * (z_up - z_down)
                    else:
                        beside = x_up + x_down
                        beside = beside + y_up + y_down
                        beside = beside + z_up + z_down
                        value = beside - 6.0 * center
                    put(q, t, value)


def products_kernel(
    scale,
    adjoint_ref,
    direct_ref,
    weight_ref,
    weighted_hbm,
    out_hbm,
    gram_ref,
    parts_ref,
    weighted_ref,
    out_ref,
    sems,
):
    fetch = pltpu.make_async_copy(weighted_hbm, weighted_ref, sems.at[2])
    fetch.start()
    stores = [
        pltpu.make_async_copy(out_ref.at[:, rows], out_hbm.at[:, rows], sems.at[n])
        for n, rows in enumerate((pl.ds(0, 64), pl.ds(64, 64)))
    ]
    transposed = (((1,), (1,)), ((), ()))
    weight = weight_ref[...]
    gram = jnp.zeros((M, M), jnp.float32)
    for comp in range(COMPONENTS):
        for t in range(0, TILES, 2):
            adjoint = columns(adjoint_ref, comp, (t, t + 1))
            direct = columns(direct_ref, comp, (t, t + 1))
            gram = gram + lax.dot_general(
                direct, adjoint, transposed, preferred_element_type=jnp.float32
            )
            modes = jnp.dot(weight, adjoint, preferred_element_type=jnp.float32)
            high = modes.astype(jnp.bfloat16)
            rest = modes - high.astype(jnp.float32)
            middle = rest.astype(jnp.bfloat16)
            low = (rest - middle.astype(jnp.float32)).astype(jnp.bfloat16)
            for part, value in enumerate((high, middle, low)):
                parts_ref[comp, part * R : (part + 1) * R, t * NZ : (t + 2) * NZ] = value
    gram = gram * scale
    gram_ref[0] = gram[:, :NZ]
    gram_ref[1] = gram[:, NZ:]
    for core in range(2):
        for snap in range(SNAP):
            half, at = snap // 2, (snap % 2) * COLS
            halves = [
                gram_ref[half, pl.ds(2 * core + t, M // 4, stride=4), :][:, at : at + COLS]
                for t in range(2)
            ]
            out_ref[core * SNAP + snap, :64, :] = jnp.concatenate(halves, axis=1)
    stores[0].start()
    blocks = []
    row = 0
    fetch.wait()
    for target, members in enumerate(MEMBERS):
        count = len(members) * R
        product = lax.dot_general(
            parts_ref[target],
            weighted_ref[row : row + count, :],
            transposed,
            preferred_element_type=jnp.float32,
        )
        row += count
        blocks.append((product[:R] + (product[R : 2 * R] + product[2 * R :])) * scale)
    for snap in range(SNAP):
        own = jnp.concatenate(
            [
                block[:, snap * (block.shape[1] // SNAP) : (snap + 1) * (block.shape[1] // SNAP)]
                for block in blocks
            ],
            axis=1,
        )
        for core in range(2):
            for w in range(4):
                rows = own[(2 * w + core) * 8 : (2 * w + core + 1) * 8]
                out_ref[core * SNAP + snap, 64 + w * 8 : 64 + w * 8 + 8, :] = rows[:, :NZ]
                out_ref[core * SNAP + snap, 96 + w * 8 : 96 + w * 8 + 8, :] = rows[:, NZ:]
    stores[1].start()
    for store in stores:
        store.wait()


def call(kernel, out_shape, flops, moved, scratch=(), inputs=None, outputs=None, limit=LIMIT):
    def run(*operands):
        spaces = dict.fromkeys(range(len(operands)), pltpu.VMEM) | (inputs or {})
        results = pl.BlockSpec(memory_space=outputs or pltpu.VMEM)
        several = isinstance(out_shape, tuple)
        return pl.pallas_call(
            kernel,
            out_shape=out_shape,
            in_specs=[pl.BlockSpec(memory_space=space) for space in spaces.values()],
            out_specs=[results] * len(out_shape) if several else results,
            scratch_shapes=list(scratch),
            compiler_params=pltpu.CompilerParams(vmem_limit_bytes=limit),
            cost_estimate=pl.CostEstimate(flops=flops, bytes_accessed=moved, transcendentals=0),
        )(*operands)

    return run


def shards(direct_snaps, adjoint_snaps, left_factor, right_factor, singular, term_coeff, term_slot):
    scale = 1.0 / math.sqrt(1572864)
    left = mode_weight(left_factor, singular).T
    right = mode_weight(right_factor, singular).T
    tiles = COMPONENTS * TILES

    def shape(*dims, dtype=jnp.bfloat16):
        return jax.ShapeDtypeStruct(dims, dtype)

    spread_shape = shape(SNAP, tiles, COLS, NZ)
    ready = call(
        direct_kernel,
        spread_shape,
        0,
        3 << 20,
        (
            pltpu.VMEM((12, COLS, NY, NZ), jnp.bfloat16),
            pltpu.VMEM((SNAP, tiles, COLS, NZ), jnp.bfloat16),
            pltpu.SemaphoreType.DMA((12,)),
            pltpu.SemaphoreType.DMA((12,)),
        ),
        {0: pl.ANY},
        pl.ANY,
        WHOLE,
    )(direct_snaps)
    direct = lax.all_to_all(ready, "snap", 0, 0, tiled=True)
    here = lax.axis_index("snap").astype(jnp.int32).reshape(1)
    ready, adjoint_weight, direct_weight, coeff = call(
        adjoint_kernel,
        (
            spread_shape,
            shape(R, M),
            shape(R, M),
            shape(TERMS, TILES, NZ, dtype=jnp.float32),
        ),
        0,
        3 << 20,
        inputs={0: pltpu.SMEM},
    )(here, adjoint_snaps, left, right, term_coeff)
    adjoint = lax.all_to_all(ready, "snap", 0, 0, tiled=True)
    odd = jnp.stack([lax.axis_index("core"), lax.axis_index("snap") % 2]).astype(jnp.int32)
    modes, *edges = call(
        modes_kernel,
        (shape(tiles, R, NZ), shape(6, R, NZ), shape(6, R, NZ), shape(R, NZ), shape(R, NZ)),
        2 * R * M * 3 * CELLS,
        2 << 20,
        inputs={0: pltpu.SMEM},
    )(odd, direct, direct_weight)

    def swap(array, axis, count, start):
        pairs = [(i, i + 1) for i in range(start, count - 1, 2)]
        return lax.ppermute(array, axis, pairs + [(j, i) for i, j in pairs])

    x_near = swap(edges[0], SPACE, 128, 0)
    z_near = swap(edges[2], "snap", SNAP, 0)
    x_far = swap(edges[1], SPACE, 128, 1)
    z_far = swap(edges[3], "snap", SNAP, 1)
    weighted = call(
        weighted_kernel,
        pltpu.HBM((TERMS * R, CELLS), jnp.bfloat16),
        1 << 26,
        3 << 20,
        inputs={0: pltpu.SMEM},
    )(odd, modes, x_near, x_far, z_near, z_far, coeff)
    terms = call(
        functools.partial(products_kernel, scale),
        pltpu.HBM((CHUNKS, 128, NZ), jnp.float32),
        1 << 30,
        6 << 20,
        (
            pltpu.VMEM((2, M, NZ), jnp.float32),
            pltpu.VMEM((COMPONENTS, 3 * R, CELLS), jnp.bfloat16),
            pltpu.VMEM((TERMS * R, CELLS), jnp.bfloat16),
            pltpu.VMEM((CHUNKS, 128, NZ), jnp.float32),
            pltpu.SemaphoreType.DMA((3,)),
        ),
        {3: pltpu.HBM},
        pltpu.HBM,
    )(adjoint, direct, adjoint_weight, pltpu.with_memory_space_constraint(weighted, pltpu.HBM))
    near = lax.all_to_all(terms, ("core", "snap"), 0, 0, tiled=True).sum(axis=0)
    gram = near[:64]
    operators = near[64:].reshape(2, 4, 8, 8, OWN).transpose(0, 3, 1, 2, 4).reshape(TERMS, 4 * NZ)
    selector = (
        term_slot[jnp.array(ORDER)][None, :] == jnp.arange(TERMS, dtype=jnp.int32)[:, None]
    ).astype(jnp.float32)
    ordered = jnp.dot(selector, operators, precision=lax.Precision.HIGHEST)
    owned = jnp.stack([gram, ordered.reshape(64, NZ)], axis=1)
    final = lax.all_to_all(owned, ("z", "y"), 0, 0, tiled=True).sum(axis=0)
    return (final[0].reshape(2, COLS).T, final[1].reshape(8, OWN))


def solution(mesh):
    parts = Mesh(mesh.devices.reshape(8, 8, 2, 4), SPACE + ("snap",))
    return jax.shard_map(
        shards,
        mesh=parts,
        in_specs=(
            P("snap", None, SPACE, None, None),
            P("snap", None, SPACE, None, None),
            P(),
            P(),
            P(),
            P(None, SPACE, None, None),
            P(),
        ),
        out_specs=(P("snap", SPACE), P(SPACE, "snap")),
        check_vma=False,
    )
```

```python
import functools
import math

import jax
import jax.numpy as jnp
from jax import lax
from jax.experimental import pallas as pl
from jax.experimental.pallas import tpu as pltpu
from jax.sharding import Mesh, PartitionSpec as P

stencil_kind = (4, 4, 4, 1, 2, 3, 1, 2, 3, 1, 2, 3, 0, 0, 0, 0)
source_comp = (0, 1, 2, 0, 0, 0, 1, 1, 1, 2, 2, 2, 0, 1, 2, 1)
target_comp = (0, 1, 2, 0, 0, 0, 1, 1, 1, 2, 2, 2, 1, 2, 0, 0)
TERMS = len(stencil_kind)
COMPONENTS = 3
MEMBERS = tuple(
    tuple(q for q in range(TERMS) if target_comp[q] == target) for target in range(COMPONENTS)
)
ORDER = tuple(q for members in MEMBERS for q in members)
M = 256
R = 64
NY = 8
NZ = 128
CELLS = NY * NZ
SNAP = 4
COLS = M // SNAP
OWN = R // SNAP
SPACE = ("z", "y", "core")
CHUNKS = 8
PIECES = 4
LIMIT = 24 * 1024 * 1024
WHOLE = 60 * 1024 * 1024


def mode_weight(factor, singular):
    return (factor / jnp.sqrt(singular)[None, :]).astype(jnp.bfloat16)


TILES = 8
GROUP = NZ // SNAP


def spread_rows(layer, out_ref, first, at):
    rows = jnp.swapaxes(layer, 0, 1)
    for half in range(2):
        group = [rows[half * 4 + i] for i in range(4)]
        for quarter in range(SNAP):
            lanes = slice(quarter * GROUP, (quarter + 1) * GROUP)
            out_ref[quarter, first + half, at : at + layer.shape[0]] = jnp.concatenate(
                [row[:, lanes] for row in group], axis=1
            )


def direct_kernel(snaps_ref, out_ref, raw, spread, arrived, sent):
    count = COLS // PIECES
    parts = [pl.ds(n * count, count) for n in range(PIECES)]
    arrivals = [
        pltpu.make_async_copy(snaps_ref.at[part], raw.at[part], arrived.at[n])
        for n, part in enumerate(parts)
    ]
    for copy in arrivals:
        copy.start()
    departures = []
    for n, part in enumerate(parts):
        arrivals[n].wait()
        for comp in range(COMPONENTS):
            for x in range(4):
                spread_rows(raw[part, comp, x], spread, comp * TILES + x * 2, n * count)
        departures.append(
            pltpu.make_async_copy(spread.at[:, :, part], out_ref.at[:, :, part], sent.at[n])
        )
        departures[-1].start()
    for copy in departures:
        copy.wait()


def adjoint_kernel(
    snap_ref, snaps_ref, left_ref, right_ref, coeff_ref, out_ref, left_out, right_out, coeff_out
):
    for comp in range(COMPONENTS):
        for x in range(4):
            spread_rows(snaps_ref[:, comp, x], out_ref, comp * TILES + x * 2, 0)
    left_out[...] = left_ref[...]
    right_out[...] = right_ref[...]
    shift = lax.rem(NZ - GROUP * snap_ref[0], NZ)
    for q in range(TERMS):
        for x in range(4):
            own = pltpu.roll(coeff_ref[q, x], shift, 1)
            for half in range(2):
                coeff_out[q, x * 2 + half : x * 2 + half + 1, :] = jnp.concatenate(
                    [own[half * 4 + i : half * 4 + i + 1, :GROUP] for i in range(4)], axis=1
                )


def columns(ref, comp, tiles):
    return jnp.concatenate(
        [
            jnp.concatenate([ref[s, comp * TILES + t] for s in range(SNAP)], axis=0)
            for t in tiles
        ],
        axis=1,
    )


def modes_kernel(
    odd_ref, snaps_ref, weight_ref, out_ref, x_near_ref, x_far_ref, z_near_ref, z_far_ref
):
    x_odd = odd_ref[0] == 1
    z_odd = odd_ref[1] == 1
    weight = weight_ref[...]
    place = lax.rem(lax.broadcasted_iota(jnp.int32, (R, NZ), 1), GROUP)
    low = jnp.zeros((R, NZ), jnp.float32)
    high = jnp.zeros((R, NZ), jnp.float32)
    first, last = [], []
    for comp in range(COMPONENTS):
        for t in range(0, TILES, 2):
            block = columns(snaps_ref, comp, (t, t + 1))
            modes = jnp.dot(weight, block, preferred_element_type=jnp.float32)
            modes = modes.astype(jnp.bfloat16)
            for half in range(2):
                tile = modes[:, half * NZ : (half + 1) * NZ]
                index = comp * TILES + t + half
                out_ref[index] = tile
                if t == 0:
                    first.append(tile)
                if t == TILES - 2:
                    last.append(tile)
                wide = tile.astype(jnp.float32)
                edge = jnp.where(place == 0, wide, 0.0)
                low = low + (pltpu.roll(edge, index, 1) if index else edge)
                edge = jnp.where(place == GROUP - 1, wide, 0.0)
                high = high + pltpu.roll(edge, NZ + index - (GROUP - 1), 1)
    z_near_ref[...] = jnp.where(z_odd, low, high).astype(jnp.bfloat16)
    z_far_ref[...] = jnp.where(z_odd, high, low).astype(jnp.bfloat16)
    for n in range(6):
        x_near_ref[n] = jnp.where(x_odd, first[n], last[n])
        x_far_ref[n] = jnp.where(x_odd, last[n], first[n])


def weighted_terms(comp, modes_ref, before, after, below, above, coeff_ref, out_ref):
    lane = lax.broadcasted_iota(jnp.int32, (R, NZ), 1)
    place = lax.rem(lane, GROUP)
    base = [0]
    for members in MEMBERS:
        base.append(base[-1] + len(members) * R)

    def put(q, t, value):
        target = target_comp[q]
        count = len(MEMBERS[target])
        at = MEMBERS[target].index(q)
        value = (value * coeff_ref[q, t : t + 1, :]).astype(jnp.bfloat16)
        for block in range(SNAP):
            row = base[target] + (block * count + at) * OWN
            out_ref[row : row + OWN, t * NZ : (t + 1) * NZ] = value[block * OWN : (block + 1) * OWN]

    field = [modes_ref[comp * TILES + t].astype(jnp.float32) for t in range(TILES)]
    down = before[comp * 2 : comp * 2 + 2] + field[:-2]
    up = field[2:] + after[comp * 2 : comp * 2 + 2]
    for x in range(4):
        pair = field[2 * x : 2 * x + 2]
        ahead = [pltpu.roll(v, NZ - GROUP, 1) for v in pair]
        behind = [pltpu.roll(v, GROUP, 1) for v in pair]
        for half in range(2):
            t = 2 * x + half
            index = comp * TILES + t
            center = pair[half]
            x_up, x_down = up[t], down[t]
            y_up = jnp.where(lane >= NZ - GROUP, ahead[1] if half == 0 else 0.0, ahead[half])
            y_down = jnp.where(lane < GROUP, behind[0] if half == 1 else 0.0, behind[half])
            z_up = jnp.where(
                place == GROUP - 1,
                pltpu.roll(above, GROUP - 1 - index, 1),
                pltpu.roll(center, NZ - 1, 1),
            )
            z_down = jnp.where(
                place == 0,
                pltpu.roll(below, NZ - index, 1) if index else below,
                pltpu.roll(center, 1, 1),
            )
            for q in range(TERMS):
                if source_comp[q] != comp:
                    continue
                kind = stencil_kind[q]
                if kind == 0:
                    value = center
                elif kind == 1:
                    value = 0.5 * (x_up - x_down)
                elif kind == 2:
                    value = 0.5 * (y_up - y_down)
                elif kind == 3:
                    value = 0.5 * (z_up - z_down)
                else:
                    beside = x_up + x_down
                    beside = beside + y_up + y_down
                    beside = beside + z_up + z_down
                    value = beside - 6.0 * center
                put(q, t, value)


def products_kernel(
    scale,
    odd_ref,
    adjoint_ref,
    direct_ref,
    *refs,
):
    sources, (out_hbm, gram_ref, parts_ref, weighted_ref, out_ref, *held, sems, fetched) = refs[:7], refs[7:]
    fetches = [
        pltpu.make_async_copy(source, target, fetched.at[n])
        for n, (source, target) in enumerate(zip(sources, held))
    ]
    for fetch in fetches:
        fetch.start()
    weight_ref, modes_ref, x_near_ref, x_far_ref, z_near_ref, z_far_ref, coeff_ref = held
    stores = [
        pltpu.make_async_copy(out_ref.at[:, rows], out_hbm.at[:, rows], sems.at[n])
        for n, rows in enumerate((pl.ds(0, 64), pl.ds(64, 64)))
    ]
    transposed = (((1,), (1,)), ((), ()))
    gram = jnp.zeros((M, M), jnp.float32)
    for comp in range(COMPONENTS):
        for t in range(0, TILES, 2):
            gram = gram + lax.dot_general(
                columns(direct_ref, comp, (t, t + 1)),
                columns(adjoint_ref, comp, (t, t + 1)),
                transposed,
                preferred_element_type=jnp.float32,
            )
    for fetch in fetches:
        fetch.wait()
    x_odd = odd_ref[0] == 1
    z_odd = odd_ref[1] == 1
    z_near = z_near_ref[...].astype(jnp.float32)
    z_far = z_far_ref[...].astype(jnp.float32)
    below = jnp.where(z_odd, z_near, z_far)
    above = jnp.where(z_odd, z_far, z_near)
    x_near = [x_near_ref[n].astype(jnp.float32) for n in range(6)]
    x_far = [x_far_ref[n].astype(jnp.float32) for n in range(6)]
    before = [jnp.where(x_odd, near, far) for near, far in zip(x_near, x_far)]
    after = [jnp.where(x_odd, far, near) for near, far in zip(x_near, x_far)]
    weight = weight_ref[...]
    for comp in range(COMPONENTS):
        for t in range(0, TILES, 2):
            adjoint = columns(adjoint_ref, comp, (t, t + 1))
            modes = jnp.dot(weight, adjoint, preferred_element_type=jnp.float32)
            high = modes.astype(jnp.bfloat16)
            rest = modes - high.astype(jnp.float32)
            middle = rest.astype(jnp.bfloat16)
            low = (rest - middle.astype(jnp.float32)).astype(jnp.bfloat16)
            for part, value in enumerate((high, middle, low)):
                parts_ref[comp, part * R : (part + 1) * R, t * NZ : (t + 2) * NZ] = value
        weighted_terms(comp, modes_ref, before, after, below, above, coeff_ref, weighted_ref)
    gram = gram * scale
    gram_ref[0] = gram[:, :NZ]
    gram_ref[1] = gram[:, NZ:]
    for core in range(2):
        for snap in range(SNAP):
            half, at = snap // 2, (snap % 2) * COLS
            halves = [
                gram_ref[half, pl.ds(2 * core + t, M // 4, stride=4), :][:, at : at + COLS]
                for t in range(2)
            ]
            out_ref[core * SNAP + snap, :64, :] = jnp.concatenate(halves, axis=1)
    stores[0].start()
    blocks = []
    row = 0
    for target, members in enumerate(MEMBERS):
        count = len(members) * R
        product = lax.dot_general(
            parts_ref[target],
            weighted_ref[row : row + count, :],
            transposed,
            preferred_element_type=jnp.float32,
        )
        row += count
        blocks.append((product[:R] + (product[R : 2 * R] + product[2 * R :])) * scale)
    for snap in range(SNAP):
        own = jnp.concatenate(
            [
                block[:, snap * (block.shape[1] // SNAP) : (snap + 1) * (block.shape[1] // SNAP)]
                for block in blocks
            ],
            axis=1,
        )
        for core in range(2):
            for w in range(4):
                rows = own[(2 * w + core) * 8 : (2 * w + core + 1) * 8]
                out_ref[core * SNAP + snap, 64 + w * 8 : 64 + w * 8 + 8, :] = rows[:, :NZ]
                out_ref[core * SNAP + snap, 96 + w * 8 : 96 + w * 8 + 8, :] = rows[:, NZ:]
    stores[1].start()
    for store in stores:
        store.wait()


def finish_kernel(sums_ref, gram_ref, reduced_ref):
    total = jnp.sum(sums_ref[...], axis=0)
    gram_ref[...] = jnp.concatenate([total[0:1, :COLS], total[0:1, COLS:]], axis=0)
    reduced_ref[...] = jnp.concatenate(
        [total[1:2, v * OWN : (v + 1) * OWN] for v in range(8)], axis=0
    )


def call(kernel, out_shape, flops, moved, scratch=(), inputs=None, outputs=None, limit=LIMIT):
    def run(*operands):
        spaces = dict.fromkeys(range(len(operands)), pltpu.VMEM) | (inputs or {})
        results = pl.BlockSpec(memory_space=outputs or pltpu.VMEM)
        several = isinstance(out_shape, tuple)
        return pl.pallas_call(
            kernel,
            out_shape=out_shape,
            in_specs=[pl.BlockSpec(memory_space=space) for space in spaces.values()],
            out_specs=[results] * len(out_shape) if several else results,
            scratch_shapes=list(scratch),
            compiler_params=pltpu.CompilerParams(vmem_limit_bytes=limit),
            cost_estimate=pl.CostEstimate(flops=flops, bytes_accessed=moved, transcendentals=0),
        )(*operands)

    return run


def shards(direct_snaps, adjoint_snaps, left_factor, right_factor, singular, term_coeff, term_slot):
    scale = 1.0 / math.sqrt(1572864)
    left = mode_weight(left_factor, singular).T
    right = mode_weight(right_factor, singular).T
    tiles = COMPONENTS * TILES

    def shape(*dims, dtype=jnp.bfloat16):
        return jax.ShapeDtypeStruct(dims, dtype)

    spread_shape = shape(SNAP, tiles, COLS, NZ)
    ready = call(
        direct_kernel,
        pltpu.HBM(spread_shape.shape, jnp.bfloat16),
        0,
        3 << 20,
        (
            pltpu.VMEM(direct_snaps.shape, jnp.bfloat16),
            pltpu.VMEM((SNAP, tiles, COLS, NZ), jnp.bfloat16),
            pltpu.SemaphoreType.DMA((PIECES,)),
            pltpu.SemaphoreType.DMA((PIECES,)),
        ),
        {0: pl.ANY},
        pltpu.HBM,
        WHOLE,
    )(direct_snaps)
    direct = lax.all_to_all(ready, "snap", 0, 0, tiled=True)
    here = lax.axis_index("snap").astype(jnp.int32).reshape(1)
    ready, adjoint_weight, direct_weight, coeff = call(
        adjoint_kernel,
        (
            spread_shape,
            pltpu.HBM((R, M), jnp.bfloat16),
            pltpu.HBM((R, M), jnp.bfloat16),
            pltpu.HBM((TERMS, TILES, NZ), jnp.float32),
        ),
        0,
        3 << 20,
        inputs={0: pltpu.SMEM},
    )(here, adjoint_snaps, left, right, term_coeff)
    adjoint = lax.all_to_all(ready, "snap", 0, 0, tiled=True)
    odd = jnp.stack([lax.axis_index("core"), lax.axis_index("snap") % 2]).astype(jnp.int32)
    modes, *edges = call(
        modes_kernel,
        (shape(tiles, R, NZ), shape(6, R, NZ), shape(6, R, NZ), shape(R, NZ), shape(R, NZ)),
        2 * R * M * 3 * CELLS,
        2 << 20,
        inputs={0: pltpu.SMEM},
    )(odd, direct, direct_weight)

    def swap(array, axis, count, start):
        pairs = [(i, i + 1) for i in range(start, count - 1, 2)]
        return lax.ppermute(array, axis, pairs + [(j, i) for i, j in pairs])

    x_near = swap(edges[0], SPACE, 128, 0)
    z_near = swap(edges[2], "snap", SNAP, 0)
    x_far = swap(edges[1], SPACE, 128, 1)
    z_far = swap(edges[3], "snap", SNAP, 1)
    adjoint_weight, coeff = (
        pltpu.with_memory_space_constraint(array, pltpu.HBM) for array in (adjoint_weight, coeff)
    )
    fetched = (adjoint_weight, modes, x_near, x_far, z_near, z_far, coeff)
    terms = call(
        functools.partial(products_kernel, scale),
        pltpu.HBM((CHUNKS, 128, NZ), jnp.float32),
        1 << 30,
        6 << 20,
        (
            pltpu.VMEM((2, M, NZ), jnp.float32),
            pltpu.VMEM((COMPONENTS, 3 * R, CELLS), jnp.bfloat16),
            pltpu.VMEM((TERMS * R, CELLS), jnp.bfloat16),
            pltpu.VMEM((CHUNKS, 128, NZ), jnp.float32),
            *(pltpu.VMEM(array.shape, array.dtype) for array in fetched),
            pltpu.SemaphoreType.DMA((2,)),
            pltpu.SemaphoreType.DMA((len(fetched),)),
        ),
        {0: pltpu.SMEM} | dict.fromkeys(range(3, 3 + len(fetched)), pl.ANY),
        pltpu.HBM,
    )(odd, adjoint, direct, *fetched)
    near = lax.all_to_all(terms, ("core", "snap"), 0, 0, tiled=True).sum(axis=0)
    gram = near[:64]
    operators = near[64:].reshape(2, 4, 8, 8, OWN).transpose(0, 3, 1, 2, 4).reshape(TERMS, 4 * NZ)
    selector = (
        term_slot[jnp.array(ORDER)][None, :] == jnp.arange(TERMS, dtype=jnp.int32)[:, None]
    ).astype(jnp.float32)
    ordered = jnp.dot(selector, operators, precision=lax.Precision.HIGHEST)
    owned = jnp.stack([gram, ordered.reshape(64, NZ)], axis=1)
    sums = lax.all_to_all(owned, ("z", "y"), 0, 0, tiled=True)
    outs = (shape(2, COLS, dtype=jnp.float32), shape(8, OWN, dtype=jnp.float32))
    gram, reduced = call(finish_kernel, outs, 0, 1 << 16)(sums)
    return (gram.T, reduced)


def solution(mesh):
    parts = Mesh(mesh.devices.reshape(8, 8, 2, 4), SPACE + ("snap",))
    return jax.shard_map(
        shards,
        mesh=parts,
        in_specs=(
            P("snap", None, SPACE, None, None),
            P("snap", None, SPACE, None, None),
            P(),
            P(),
            P(),
            P(None, SPACE, None, None),
            P(),
        ),
        out_specs=(P("snap", SPACE), P(SPACE, "snap")),
        check_vma=False,
    )
```

```python
import functools
import math

import jax
import jax.numpy as jnp
from jax import lax
from jax.experimental import pallas as pl
from jax.experimental.pallas import tpu as pltpu
from jax.sharding import Mesh, PartitionSpec as P

stencil_kind = (4, 4, 4, 1, 2, 3, 1, 2, 3, 1, 2, 3, 0, 0, 0, 0)
source_comp = (0, 1, 2, 0, 0, 0, 1, 1, 1, 2, 2, 2, 0, 1, 2, 1)
target_comp = (0, 1, 2, 0, 0, 0, 1, 1, 1, 2, 2, 2, 1, 2, 0, 0)
TERMS = len(stencil_kind)
COMPONENTS = 3
MEMBERS = tuple(
    tuple(q for q in range(TERMS) if target_comp[q] == target) for target in range(COMPONENTS)
)
ORDER = tuple(q for members in MEMBERS for q in members)
M = 256
R = 64
NY = 8
NZ = 128
CELLS = NY * NZ
SNAP = 4
COLS = M // SNAP
OWN = R // SNAP
SPACE = ("z", "y", "core")
CHUNKS = 8
PIECES = 4
LIMIT = 24 * 1024 * 1024
WHOLE = 60 * 1024 * 1024


def mode_weight(factor, singular):
    return (factor / jnp.sqrt(singular)[None, :]).astype(jnp.bfloat16)


TILES = 8
GROUP = NZ // SNAP
WEIGHT_AT = COMPONENTS * TILES
COEFF_AT = WEIGHT_AT + 2
HELD = COEFF_AT + 2


def spread_rows(layer, out_ref, first, at):
    rows = jnp.swapaxes(layer, 0, 1)
    for half in range(2):
        group = [rows[half * 4 + i] for i in range(4)]
        for quarter in range(SNAP):
            lanes = slice(quarter * GROUP, (quarter + 1) * GROUP)
            out_ref[quarter, first + half, at : at + layer.shape[0]] = jnp.concatenate(
                [row[:, lanes] for row in group], axis=1
            )


def direct_kernel(snaps_ref, out_ref, raw, spread, arrived, sent):
    count = COLS // PIECES
    parts = [pl.ds(n * count, count) for n in range(PIECES)]
    arrivals = [
        pltpu.make_async_copy(snaps_ref.at[part], raw.at[part], arrived.at[n])
        for n, part in enumerate(parts)
    ]
    for copy in arrivals:
        copy.start()
    departures = []
    for n, part in enumerate(parts):
        arrivals[n].wait()
        for comp in range(COMPONENTS):
            for x in range(4):
                spread_rows(raw[part, comp, x], spread, comp * TILES + x * 2, n * count)
        departures.append(
            pltpu.make_async_copy(spread.at[:, :, part], out_ref.at[:, :, part], sent.at[n])
        )
        departures[-1].start()
    for copy in departures:
        copy.wait()


def adjoint_kernel(
    snap_ref, snaps_ref, left_ref, right_ref, coeff_ref, out_ref, left_out, right_out, coeff_out
):
    for comp in range(COMPONENTS):
        for x in range(4):
            spread_rows(snaps_ref[:, comp, x], out_ref, comp * TILES + x * 2, 0)
    left_out[...] = left_ref[...]
    right_out[...] = right_ref[...]
    shift = lax.rem(NZ - GROUP * snap_ref[0], NZ)
    for q in range(TERMS):
        for x in range(4):
            own = pltpu.roll(coeff_ref[q, x], shift, 1)
            for half in range(2):
                row = q * TILES + x * 2 + half
                coeff_out[row : row + 1, :] = jnp.concatenate(
                    [own[half * 4 + i : half * 4 + i + 1, :GROUP] for i in range(4)], axis=1
                )


def columns(ref, comp, tiles):
    return jnp.concatenate(
        [
            jnp.concatenate([ref[s, comp * TILES + t] for s in range(SNAP)], axis=0)
            for t in tiles
        ],
        axis=1,
    )


def modes_kernel(
    snaps_ref,
    weight_ref,
    adjoint_weight_ref,
    coeff_ref,
    held_ref,
    first_ref,
    last_ref,
    low_ref,
    high_ref,
):
    for n in range(2):
        wide = adjoint_weight_ref[:, n * NZ : (n + 1) * NZ].astype(jnp.float32)
        held_ref[WEIGHT_AT + n] = wide
        held_ref[COEFF_AT + n] = coeff_ref[n * R : (n + 1) * R, :]
    weight = weight_ref[...]
    place = lax.rem(lax.broadcasted_iota(jnp.int32, (R, NZ), 1), GROUP)
    low = jnp.zeros((R, NZ), jnp.float32)
    high = jnp.zeros((R, NZ), jnp.float32)
    for comp in range(COMPONENTS):
        for t in range(0, TILES, 2):
            block = columns(snaps_ref, comp, (t, t + 1))
            modes = jnp.dot(weight, block, preferred_element_type=jnp.float32)
            modes = modes.astype(jnp.bfloat16)
            for half in range(2):
                tile = modes[:, half * NZ : (half + 1) * NZ]
                index = comp * TILES + t + half
                wide = tile.astype(jnp.float32)
                held_ref[index] = wide
                if t == 0:
                    first_ref[comp * 2 + half] = tile
                if t == TILES - 2:
                    last_ref[comp * 2 + half] = tile
                edge = jnp.where(place == 0, wide, 0.0)
                low = low + (pltpu.roll(edge, index, 1) if index else edge)
                edge = jnp.where(place == GROUP - 1, wide, 0.0)
                high = high + pltpu.roll(edge, NZ + index - (GROUP - 1), 1)
    low_ref[...] = low.astype(jnp.bfloat16)
    high_ref[...] = high.astype(jnp.bfloat16)


def weighted_terms(comp, held_ref, before, after, below, above, out_ref):
    lane = lax.broadcasted_iota(jnp.int32, (R, NZ), 1)
    place = lax.rem(lane, GROUP)
    base = [0]
    for members in MEMBERS:
        base.append(base[-1] + len(members) * R)

    def put(q, t, value):
        target = target_comp[q]
        count = len(MEMBERS[target])
        at = MEMBERS[target].index(q)
        row = (q * TILES + t) % R
        coeff = held_ref[COEFF_AT + q * TILES // R, row : row + 1, :]
        value = (value * coeff).astype(jnp.bfloat16)
        for block in range(SNAP):
            row = base[target] + (block * count + at) * OWN
            out_ref[row : row + OWN, t * NZ : (t + 1) * NZ] = value[block * OWN : (block + 1) * OWN]

    field = [held_ref[comp * TILES + t] for t in range(TILES)]
    down = before[comp * 2 : comp * 2 + 2] + field[:-2]
    up = field[2:] + after[comp * 2 : comp * 2 + 2]
    for x in range(4):
        pair = field[2 * x : 2 * x + 2]
        ahead = [pltpu.roll(v, NZ - GROUP, 1) for v in pair]
        behind = [pltpu.roll(v, GROUP, 1) for v in pair]
        for half in range(2):
            t = 2 * x + half
            index = comp * TILES + t
            center = pair[half]
            x_up, x_down = up[t], down[t]
            y_up = jnp.where(lane >= NZ - GROUP, ahead[1] if half == 0 else 0.0, ahead[half])
            y_down = jnp.where(lane < GROUP, behind[0] if half == 1 else 0.0, behind[half])
            z_up = jnp.where(
                place == GROUP - 1,
                pltpu.roll(above, GROUP - 1 - index, 1),
                pltpu.roll(center, NZ - 1, 1),
            )
            z_down = jnp.where(
                place == 0,
                pltpu.roll(below, NZ - index, 1) if index else below,
                pltpu.roll(center, 1, 1),
            )
            for q in range(TERMS):
                if source_comp[q] != comp:
                    continue
                kind = stencil_kind[q]
                if kind == 0:
                    value = center
                elif kind == 1:
                    value = 0.5 * (x_up - x_down)
                elif kind == 2:
                    value = 0.5 * (y_up - y_down)
                elif kind == 3:
                    value = 0.5 * (z_up - z_down)
                else:
                    beside = x_up + x_down
                    beside = beside + y_up + y_down
                    beside = beside + z_up + z_down
                    value = beside - 6.0 * center
                put(q, t, value)


def products_kernel(
    scale,
    adjoint_ref,
    direct_ref,
    held_hbm,
    before_ref,
    after_ref,
    below_ref,
    above_ref,
    out_hbm,
    held_ref,
    gram_ref,
    parts_ref,
    weighted_ref,
    out_ref,
    sems,
):
    fetch = pltpu.make_async_copy(held_hbm, held_ref, sems.at[2])
    fetch.start()
    stores = [
        pltpu.make_async_copy(out_ref.at[:, rows], out_hbm.at[:, rows], sems.at[n])
        for n, rows in enumerate((pl.ds(0, 64), pl.ds(64, 64)))
    ]
    transposed = (((1,), (1,)), ((), ()))
    gram = jnp.zeros((M, M), jnp.float32)
    for comp in range(COMPONENTS):
        for t in range(0, TILES, 2):
            gram = gram + lax.dot_general(
                columns(direct_ref, comp, (t, t + 1)),
                columns(adjoint_ref, comp, (t, t + 1)),
                transposed,
                preferred_element_type=jnp.float32,
            )
    fetch.wait()
    below = below_ref[...].astype(jnp.float32)
    above = above_ref[...].astype(jnp.float32)
    before = [before_ref[n].astype(jnp.float32) for n in range(6)]
    after = [after_ref[n].astype(jnp.float32) for n in range(6)]
    weight = jnp.concatenate([held_ref[WEIGHT_AT], held_ref[WEIGHT_AT + 1]], axis=1)
    weight = weight.astype(jnp.bfloat16)
    for comp in range(COMPONENTS):
        for t in range(0, TILES, 2):
            adjoint = columns(adjoint_ref, comp, (t, t + 1))
            modes = jnp.dot(weight, adjoint, preferred_element_type=jnp.float32)
            high = modes.astype(jnp.bfloat16)
            rest = modes - high.astype(jnp.float32)
            middle = rest.astype(jnp.bfloat16)
            low = (rest - middle.astype(jnp.float32)).astype(jnp.bfloat16)
            for part, value in enumerate((high, middle, low)):
                parts_ref[comp, part * R : (part + 1) * R, t * NZ : (t + 2) * NZ] = value
        weighted_terms(comp, held_ref, before, after, below, above, weighted_ref)
    gram = gram * scale
    gram_ref[0] = gram[:, :NZ]
    gram_ref[1] = gram[:, NZ:]
    for core in range(2):
        for snap in range(SNAP):
            half, at = snap // 2, (snap % 2) * COLS
            halves = [
                gram_ref[half, pl.ds(2 * core + t, M // 4, stride=4), :][:, at : at + COLS]
                for t in range(2)
            ]
            out_ref[core * SNAP + snap, :64, :] = jnp.concatenate(halves, axis=1)
    stores[0].start()
    blocks = []
    row = 0
    for target, members in enumerate(MEMBERS):
        count = len(members) * R
        product = lax.dot_general(
            parts_ref[target],
            weighted_ref[row : row + count, :],
            transposed,
            preferred_element_type=jnp.float32,
        )
        row += count
        blocks.append((product[:R] + (product[R : 2 * R] + product[2 * R :])) * scale)
    for snap in range(SNAP):
        own = jnp.concatenate(
            [
                block[:, snap * (block.shape[1] // SNAP) : (snap + 1) * (block.shape[1] // SNAP)]
                for block in blocks
            ],
            axis=1,
        )
        for core in range(2):
            for w in range(4):
                rows = own[(2 * w + core) * 8 : (2 * w + core + 1) * 8]
                out_ref[core * SNAP + snap, 64 + w * 8 : 64 + w * 8 + 8, :] = rows[:, :NZ]
                out_ref[core * SNAP + snap, 96 + w * 8 : 96 + w * 8 + 8, :] = rows[:, NZ:]
    stores[1].start()
    for store in stores:
        store.wait()


def finish_kernel(sums_ref, gram_ref, reduced_ref):
    total = jnp.sum(sums_ref[...], axis=0)
    gram_ref[...] = jnp.concatenate([total[0:1, :COLS], total[0:1, COLS:]], axis=0)
    reduced_ref[...] = jnp.concatenate(
        [total[1:2, v * OWN : (v + 1) * OWN] for v in range(8)], axis=0
    )


def call(kernel, out_shape, flops, moved, scratch=(), inputs=None, outputs=None, limit=LIMIT):
    def run(*operands):
        spaces = dict.fromkeys(range(len(operands)), pltpu.VMEM) | (inputs or {})
        results = pl.BlockSpec(memory_space=outputs or pltpu.VMEM)
        several = isinstance(out_shape, tuple)
        return pl.pallas_call(
            kernel,
            out_shape=out_shape,
            in_specs=[pl.BlockSpec(memory_space=space) for space in spaces.values()],
            out_specs=[results] * len(out_shape) if several else results,
            scratch_shapes=list(scratch),
            compiler_params=pltpu.CompilerParams(vmem_limit_bytes=limit),
            cost_estimate=pl.CostEstimate(flops=flops, bytes_accessed=moved, transcendentals=0),
        )(*operands)

    return run


def shards(direct_snaps, adjoint_snaps, left_factor, right_factor, singular, term_coeff, term_slot):
    scale = 1.0 / math.sqrt(1572864)
    left = mode_weight(left_factor, singular).T
    right = mode_weight(right_factor, singular).T
    tiles = COMPONENTS * TILES

    def shape(*dims, dtype=jnp.bfloat16):
        return jax.ShapeDtypeStruct(dims, dtype)

    spread_shape = shape(SNAP, tiles, COLS, NZ)
    ready = call(
        direct_kernel,
        pltpu.HBM(spread_shape.shape, jnp.bfloat16),
        0,
        3 << 20,
        (
            pltpu.VMEM(direct_snaps.shape, jnp.bfloat16),
            pltpu.VMEM((SNAP, tiles, COLS, NZ), jnp.bfloat16),
            pltpu.SemaphoreType.DMA((PIECES,)),
            pltpu.SemaphoreType.DMA((PIECES,)),
        ),
        {0: pl.ANY},
        pltpu.HBM,
        WHOLE,
    )(direct_snaps)
    direct = lax.all_to_all(ready, "snap", 0, 0, tiled=True)
    here = lax.axis_index("snap").astype(jnp.int32).reshape(1)
    ready, adjoint_weight, direct_weight, coeff = call(
        adjoint_kernel,
        (
            spread_shape,
            pltpu.HBM((R, M), jnp.bfloat16),
            pltpu.HBM((R, M), jnp.bfloat16),
            pltpu.HBM((TERMS * TILES, NZ), jnp.float32),
        ),
        0,
        3 << 20,
        inputs={0: pltpu.SMEM},
    )(here, adjoint_snaps, left, right, term_coeff)
    adjoint = lax.all_to_all(ready, "snap", 0, 0, tiled=True)
    held, first, last, low, high = call(
        modes_kernel,
        (
            pltpu.HBM((HELD, R, NZ), jnp.float32),
            shape(6, R, NZ),
            shape(6, R, NZ),
            shape(R, NZ),
            shape(R, NZ),
        ),
        2 * R * M * 3 * CELLS,
        2 << 20,
    )(direct, direct_weight, adjoint_weight, coeff)
    held = pltpu.with_memory_space_constraint(held, pltpu.HBM)
    slabs, quarters = ([(i, i + 1) for i in range(n - 1)] for n in (128, SNAP))
    before = lax.ppermute(last, SPACE, slabs)
    after = lax.ppermute(first, SPACE, [(j, i) for i, j in slabs])
    below = lax.ppermute(high, "snap", quarters)
    above = lax.ppermute(low, "snap", [(j, i) for i, j in quarters])
    terms = call(
        functools.partial(products_kernel, scale),
        pltpu.HBM((CHUNKS, 128, NZ), jnp.float32),
        1 << 30,
        6 << 20,
        (
            pltpu.VMEM((HELD, R, NZ), jnp.float32),
            pltpu.VMEM((2, M, NZ), jnp.float32),
            pltpu.VMEM((COMPONENTS, 3 * R, CELLS), jnp.bfloat16),
            pltpu.VMEM((TERMS * R, CELLS), jnp.bfloat16),
            pltpu.VMEM((CHUNKS, 128, NZ), jnp.float32),
            pltpu.SemaphoreType.DMA((3,)),
        ),
        {2: pltpu.HBM},
        pltpu.HBM,
    )(adjoint, direct, held, before, after, below, above)
    near = lax.all_to_all(terms, ("core", "snap"), 0, 0, tiled=True).sum(axis=0)
    gram = near[:64]
    operators = near[64:].reshape(2, 4, 8, 8, OWN).transpose(0, 3, 1, 2, 4).reshape(TERMS, 4 * NZ)
    selector = (
        term_slot[jnp.array(ORDER)][None, :] == jnp.arange(TERMS, dtype=jnp.int32)[:, None]
    ).astype(jnp.float32)
    ordered = jnp.dot(selector, operators, precision=lax.Precision.HIGHEST)
    owned = jnp.stack([gram, ordered.reshape(64, NZ)], axis=1)
    sums = lax.all_to_all(owned, ("z", "y"), 0, 0, tiled=True)
    outs = (shape(2, COLS, dtype=jnp.float32), shape(8, OWN, dtype=jnp.float32))
    gram, reduced = call(finish_kernel, outs, 0, 1 << 16)(sums)
    return (gram.T, reduced)


def solution(mesh):
    parts = Mesh(mesh.devices.reshape(8, 8, 2, 4), SPACE + ("snap",))
    return jax.shard_map(
        shards,
        mesh=parts,
        in_specs=(
            P("snap", None, SPACE, None, None),
            P("snap", None, SPACE, None, None),
            P(),
            P(),
            P(),
            P(None, SPACE, None, None),
            P(),
        ),
        out_specs=(P("snap", SPACE), P(SPACE, "snap")),
        check_vma=False,
    )
```

```python
import functools
import math

import jax
import jax.numpy as jnp
from jax import lax
from jax.experimental import pallas as pl
from jax.experimental.pallas import tpu as pltpu
from jax.sharding import Mesh, PartitionSpec as P

stencil_kind = (4, 4, 4, 1, 2, 3, 1, 2, 3, 1, 2, 3, 0, 0, 0, 0)
source_comp = (0, 1, 2, 0, 0, 0, 1, 1, 1, 2, 2, 2, 0, 1, 2, 1)
target_comp = (0, 1, 2, 0, 0, 0, 1, 1, 1, 2, 2, 2, 1, 2, 0, 0)
TERMS = len(stencil_kind)
COMPONENTS = 3
MEMBERS = tuple(
    tuple(q for q in range(TERMS) if target_comp[q] == target) for target in range(COMPONENTS)
)
ORDER = tuple(q for members in MEMBERS for q in members)
M = 256
R = 64
NY = 8
NZ = 128
CELLS = NY * NZ
SNAP = 4
COLS = M // SNAP
OWN = R // SNAP
SPACE = ("z", "y", "core")
PIECES = 4
LIMIT = 24 * 1024 * 1024
WHOLE = 60 * 1024 * 1024


def mode_weight(factor, singular):
    return (factor / jnp.sqrt(singular)[None, :]).astype(jnp.bfloat16)


TILES = 8
GROUP = NZ // SNAP
WEIGHT_AT = COMPONENTS * TILES
COEFF_AT = WEIGHT_AT + 2
HELD = COEFF_AT + 2


def spread_rows(layer, out_ref, first, at):
    rows = jnp.swapaxes(layer, 0, 1)
    for half in range(2):
        group = [rows[half * 4 + i] for i in range(4)]
        for quarter in range(SNAP):
            lanes = slice(quarter * GROUP, (quarter + 1) * GROUP)
            out_ref[quarter, first + half, at : at + layer.shape[0]] = jnp.concatenate(
                [row[:, lanes] for row in group], axis=1
            )


def direct_kernel(snaps_ref, out_ref, raw, spread, arrived, sent):
    count = COLS // PIECES
    parts = [pl.ds(n * count, count) for n in range(PIECES)]
    arrivals = [
        pltpu.make_async_copy(snaps_ref.at[part], raw.at[part], arrived.at[n])
        for n, part in enumerate(parts)
    ]
    for copy in arrivals:
        copy.start()
    departures = []
    for n, part in enumerate(parts):
        arrivals[n].wait()
        for comp in range(COMPONENTS):
            for x in range(4):
                spread_rows(raw[part, comp, x], spread, comp * TILES + x * 2, n * count)
        departures.append(
            pltpu.make_async_copy(spread.at[:, :, part], out_ref.at[:, :, part], sent.at[n])
        )
        departures[-1].start()
    for copy in departures:
        copy.wait()


def adjoint_kernel(
    snap_ref,
    snaps_ref,
    left_ref,
    right_ref,
    coeff_ref,
    selector_ref,
    out_ref,
    left_out,
    right_out,
    coeff_out,
    selector_out,
):
    for comp in range(COMPONENTS):
        for x in range(4):
            spread_rows(snaps_ref[:, comp, x], out_ref, comp * TILES + x * 2, 0)
    left_out[...] = left_ref[...]
    right_out[...] = right_ref[...]
    selector_out[...] = selector_ref[...]
    shift = lax.rem(NZ - GROUP * snap_ref[0], NZ)
    for q in range(TERMS):
        for x in range(4):
            own = pltpu.roll(coeff_ref[q, x], shift, 1)
            for half in range(2):
                row = q * TILES + x * 2 + half
                coeff_out[row : row + 1, :] = jnp.concatenate(
                    [own[half * 4 + i : half * 4 + i + 1, :GROUP] for i in range(4)], axis=1
                )


def columns(ref, comp, tiles):
    return jnp.concatenate(
        [
            jnp.concatenate([ref[s, comp * TILES + t] for s in range(SNAP)], axis=0)
            for t in tiles
        ],
        axis=1,
    )


def modes_kernel(
    snaps_ref,
    weight_ref,
    adjoint_weight_ref,
    coeff_ref,
    held_ref,
    first_ref,
    last_ref,
    low_ref,
    high_ref,
):
    for n in range(2):
        wide = adjoint_weight_ref[:, n * NZ : (n + 1) * NZ].astype(jnp.float32)
        held_ref[WEIGHT_AT + n] = wide
        held_ref[COEFF_AT + n] = coeff_ref[n * R : (n + 1) * R, :]
    weight = weight_ref[...]
    place = lax.rem(lax.broadcasted_iota(jnp.int32, (R, NZ), 1), GROUP)
    low = jnp.zeros((R, NZ), jnp.float32)
    high = jnp.zeros((R, NZ), jnp.float32)
    for comp in range(COMPONENTS):
        for t in range(0, TILES, 2):
            block = columns(snaps_ref, comp, (t, t + 1))
            modes = jnp.dot(weight, block, preferred_element_type=jnp.float32)
            modes = modes.astype(jnp.bfloat16)
            for half in range(2):
                tile = modes[:, half * NZ : (half + 1) * NZ]
                index = comp * TILES + t + half
                wide = tile.astype(jnp.float32)
                held_ref[index] = wide
                if t == 0:
                    first_ref[comp * 2 + half] = tile
                if t == TILES - 2:
                    last_ref[comp * 2 + half] = tile
                edge = jnp.where(place == 0, wide, 0.0)
                low = low + (pltpu.roll(edge, index, 1) if index else edge)
                edge = jnp.where(place == GROUP - 1, wide, 0.0)
                high = high + pltpu.roll(edge, NZ + index - (GROUP - 1), 1)
    low_ref[...] = low.astype(jnp.bfloat16)
    high_ref[...] = high.astype(jnp.bfloat16)


def weighted_terms(comp, held_ref, before, after, below, above, out_ref):
    lane = lax.broadcasted_iota(jnp.int32, (R, NZ), 1)
    place = lax.rem(lane, GROUP)
    base = [0]
    for members in MEMBERS:
        base.append(base[-1] + len(members) * R)

    def put(q, t, value):
        target = target_comp[q]
        count = len(MEMBERS[target])
        at = MEMBERS[target].index(q)
        row = (q * TILES + t) % R
        coeff = held_ref[COEFF_AT + q * TILES // R, row : row + 1, :]
        value = (value * coeff).astype(jnp.bfloat16)
        for block in range(SNAP):
            row = base[target] + (block * count + at) * OWN
            out_ref[row : row + OWN, t * NZ : (t + 1) * NZ] = value[block * OWN : (block + 1) * OWN]

    field = [held_ref[comp * TILES + t] for t in range(TILES)]
    down = before[comp * 2 : comp * 2 + 2] + field[:-2]
    up = field[2:] + after[comp * 2 : comp * 2 + 2]
    for x in range(4):
        pair = field[2 * x : 2 * x + 2]
        ahead = [pltpu.roll(v, NZ - GROUP, 1) for v in pair]
        behind = [pltpu.roll(v, GROUP, 1) for v in pair]
        for half in range(2):
            t = 2 * x + half
            index = comp * TILES + t
            center = pair[half]
            x_up, x_down = up[t], down[t]
            y_up = jnp.where(lane >= NZ - GROUP, ahead[1] if half == 0 else 0.0, ahead[half])
            y_down = jnp.where(lane < GROUP, behind[0] if half == 1 else 0.0, behind[half])
            z_up = jnp.where(
                place == GROUP - 1,
                pltpu.roll(above, GROUP - 1 - index, 1),
                pltpu.roll(center, NZ - 1, 1),
            )
            z_down = jnp.where(
                place == 0,
                pltpu.roll(below, NZ - index, 1) if index else below,
                pltpu.roll(center, 1, 1),
            )
            for q in range(TERMS):
                if source_comp[q] != comp:
                    continue
                kind = stencil_kind[q]
                if kind == 0:
                    value = center
                elif kind == 1:
                    value = 0.5 * (x_up - x_down)
                elif kind == 2:
                    value = 0.5 * (y_up - y_down)
                elif kind == 3:
                    value = 0.5 * (z_up - z_down)
                else:
                    beside = x_up + x_down
                    beside = beside + y_up + y_down
                    beside = beside + z_up + z_down
                    value = beside - 6.0 * center
                put(q, t, value)


def products_kernel(
    scale,
    adjoint_ref,
    direct_ref,
    held_hbm,
    before_ref,
    after_ref,
    below_ref,
    above_ref,
    keep_ref,
    send_ref,
    held_ref,
    gram_ref,
    parts_ref,
    weighted_ref,
    out_ref,
    sem,
):
    fetch = pltpu.make_async_copy(held_hbm, held_ref, sem)
    fetch.start()
    transposed = (((1,), (1,)), ((), ()))
    gram = jnp.zeros((M, M), jnp.float32)
    for comp in range(COMPONENTS):
        for t in range(0, TILES, 2):
            gram = gram + lax.dot_general(
                columns(direct_ref, comp, (t, t + 1)),
                columns(adjoint_ref, comp, (t, t + 1)),
                transposed,
                preferred_element_type=jnp.float32,
            )
    fetch.wait()
    below = below_ref[...].astype(jnp.float32)
    above = above_ref[...].astype(jnp.float32)
    before = [before_ref[n].astype(jnp.float32) for n in range(6)]
    after = [after_ref[n].astype(jnp.float32) for n in range(6)]
    weight = jnp.concatenate([held_ref[WEIGHT_AT], held_ref[WEIGHT_AT + 1]], axis=1)
    weight = weight.astype(jnp.bfloat16)
    for comp in range(COMPONENTS):
        for t in range(0, TILES, 2):
            adjoint = columns(adjoint_ref, comp, (t, t + 1))
            modes = jnp.dot(weight, adjoint, preferred_element_type=jnp.float32)
            high = modes.astype(jnp.bfloat16)
            rest = modes - high.astype(jnp.float32)
            middle = rest.astype(jnp.bfloat16)
            low = (rest - middle.astype(jnp.float32)).astype(jnp.bfloat16)
            for part, value in enumerate((high, middle, low)):
                parts_ref[comp, part * R : (part + 1) * R, t * NZ : (t + 2) * NZ] = value
        weighted_terms(comp, held_ref, before, after, below, above, weighted_ref)
    gram = gram * scale
    gram_ref[0] = gram[:, :NZ]
    gram_ref[1] = gram[:, NZ:]
    for core in range(2):
        for snap in range(SNAP):
            half, at = snap // 2, (snap % 2) * COLS
            halves = [
                gram_ref[half, pl.ds(2 * core + t, M // 4, stride=4), :][:, at : at + COLS]
                for t in range(2)
            ]
            out_ref[core * SNAP + snap, :64, :] = jnp.concatenate(halves, axis=1)
    blocks = []
    row = 0
    for target, members in enumerate(MEMBERS):
        count = len(members) * R
        product = lax.dot_general(
            parts_ref[target],
            weighted_ref[row : row + count, :],
            transposed,
            preferred_element_type=jnp.float32,
        )
        row += count
        blocks.append((product[:R] + (product[R : 2 * R] + product[2 * R :])) * scale)
    for snap in range(SNAP):
        own = jnp.concatenate(
            [
                block[:, snap * (block.shape[1] // SNAP) : (snap + 1) * (block.shape[1] // SNAP)]
                for block in blocks
            ],
            axis=1,
        )
        for core in range(2):
            for w in range(4):
                rows = own[(2 * w + core) * 8 : (2 * w + core + 1) * 8]
                out_ref[core * SNAP + snap, 64 + w * 8 : 64 + w * 8 + 8, :] = rows[:, :NZ]
                out_ref[core * SNAP + snap, 96 + w * 8 : 96 + w * 8 + 8, :] = rows[:, NZ:]
    core = lax.axis_index("core")
    keep_ref[...] = out_ref[pl.ds(core * SNAP, SNAP)]
    send_ref[...] = out_ref[pl.ds((1 - core) * SNAP, SNAP)]


def finish_kernel(sums_ref, gram_ref, reduced_ref):
    total = jnp.sum(sums_ref[...], axis=0)
    gram_ref[...] = jnp.concatenate([total[0:1, :COLS], total[0:1, COLS:]], axis=0)
    reduced_ref[...] = jnp.concatenate(
        [total[1:2, v * OWN : (v + 1) * OWN] for v in range(8)], axis=0
    )


def call(kernel, out_shape, flops, moved, scratch=(), inputs=None, outputs=None, limit=LIMIT):
    def run(*operands):
        spaces = dict.fromkeys(range(len(operands)), pltpu.VMEM) | (inputs or {})
        results = pl.BlockSpec(memory_space=outputs or pltpu.VMEM)
        several = isinstance(out_shape, tuple)
        return pl.pallas_call(
            kernel,
            out_shape=out_shape,
            in_specs=[pl.BlockSpec(memory_space=space) for space in spaces.values()],
            out_specs=[results] * len(out_shape) if several else results,
            scratch_shapes=list(scratch),
            compiler_params=pltpu.CompilerParams(vmem_limit_bytes=limit),
            cost_estimate=pl.CostEstimate(flops=flops, bytes_accessed=moved, transcendentals=0),
        )(*operands)

    return run


def shards(direct_snaps, adjoint_snaps, left_factor, right_factor, singular, term_coeff, term_slot):
    scale = 1.0 / math.sqrt(1572864)
    left = mode_weight(left_factor, singular).T
    right = mode_weight(right_factor, singular).T
    tiles = COMPONENTS * TILES

    def shape(*dims, dtype=jnp.bfloat16):
        return jax.ShapeDtypeStruct(dims, dtype)

    spread_shape = shape(SNAP, tiles, COLS, NZ)
    ready = call(
        direct_kernel,
        pltpu.HBM(spread_shape.shape, jnp.bfloat16),
        0,
        3 << 20,
        (
            pltpu.VMEM(direct_snaps.shape, jnp.bfloat16),
            pltpu.VMEM((SNAP, tiles, COLS, NZ), jnp.bfloat16),
            pltpu.SemaphoreType.DMA((PIECES,)),
            pltpu.SemaphoreType.DMA((PIECES,)),
        ),
        {0: pl.ANY},
        pltpu.HBM,
        WHOLE,
    )(direct_snaps)
    direct = lax.all_to_all(ready, "snap", 0, 0, tiled=True)
    selector = (
        term_slot[jnp.array(ORDER)][None, :] == jnp.arange(TERMS, dtype=jnp.int32)[:, None]
    ).astype(jnp.float32)
    here = lax.axis_index("snap").astype(jnp.int32).reshape(1)
    ready, adjoint_weight, direct_weight, coeff, selector = call(
        adjoint_kernel,
        (
            spread_shape,
            pltpu.HBM((R, M), jnp.bfloat16),
            pltpu.HBM((R, M), jnp.bfloat16),
            pltpu.HBM((TERMS * TILES, NZ), jnp.float32),
            pltpu.HBM((TERMS, TERMS), jnp.float32),
        ),
        0,
        3 << 20,
        inputs={0: pltpu.SMEM},
    )(here, adjoint_snaps, left, right, term_coeff, selector)
    adjoint = lax.all_to_all(ready, "snap", 0, 0, tiled=True)
    held, first, last, low, high = call(
        modes_kernel,
        (
            pltpu.HBM((HELD, R, NZ), jnp.float32),
            shape(6, R, NZ),
            shape(6, R, NZ),
            shape(R, NZ),
            shape(R, NZ),
        ),
        2 * R * M * 3 * CELLS,
        2 << 20,
    )(direct, direct_weight, adjoint_weight, coeff)
    held = pltpu.with_memory_space_constraint(held, pltpu.HBM)
    slabs, quarters = ([(i, i + 1) for i in range(n - 1)] for n in (128, SNAP))
    before = lax.ppermute(last, SPACE, slabs)
    after = lax.ppermute(first, SPACE, [(j, i) for i, j in slabs])
    below = lax.ppermute(high, "snap", quarters)
    above = lax.ppermute(low, "snap", [(j, i) for i, j in quarters])
    half = shape(SNAP, 128, NZ, dtype=jnp.float32)
    keep, send = call(
        functools.partial(products_kernel, scale),
        (half, half),
        1 << 30,
        6 << 20,
        (
            pltpu.VMEM((HELD, R, NZ), jnp.float32),
            pltpu.VMEM((2, M, NZ), jnp.float32),
            pltpu.VMEM((COMPONENTS, 3 * R, CELLS), jnp.bfloat16),
            pltpu.VMEM((TERMS * R, CELLS), jnp.bfloat16),
            pltpu.VMEM((2 * SNAP, 128, NZ), jnp.float32),
            pltpu.SemaphoreType.DMA,
        ),
        {2: pltpu.HBM},
    )(adjoint, direct, held, before, after, below, above)
    terms = keep + lax.ppermute(send, "core", [(0, 1), (1, 0)])
    near = lax.all_to_all(terms, "snap", 0, 0, tiled=True).sum(axis=0)
    gram = near[:64]
    operators = near[64:].reshape(2, 4, 8, 8, OWN).transpose(0, 3, 1, 2, 4).reshape(TERMS, 4 * NZ)
    ordered = jnp.dot(selector, operators, precision=lax.Precision.HIGHEST)
    owned = jnp.stack([gram, ordered.reshape(64, NZ)], axis=1)
    sums = lax.all_to_all(owned, ("z", "y"), 0, 0, tiled=True)
    outs = (shape(2, COLS, dtype=jnp.float32), shape(8, OWN, dtype=jnp.float32))
    gram, reduced = call(finish_kernel, outs, 0, 1 << 16)(sums)
    return (gram.T, reduced)


def solution(mesh):
    parts = Mesh(mesh.devices.reshape(8, 8, 2, 4), SPACE + ("snap",))
    return jax.shard_map(
        shards,
        mesh=parts,
        in_specs=(
            P("snap", None, SPACE, None, None),
            P("snap", None, SPACE, None, None),
            P(),
            P(),
            P(),
            P(None, SPACE, None, None),
            P(),
        ),
        out_specs=(P("snap", SPACE), P(SPACE, "snap")),
        check_vma=False,
    )
```

```python
import functools
import math

import jax
import jax.numpy as jnp
from jax import lax
from jax.experimental import pallas as pl
from jax.experimental.pallas import tpu as pltpu
from jax.sharding import Mesh, PartitionSpec as P

stencil_kind = (4, 4, 4, 1, 2, 3, 1, 2, 3, 1, 2, 3, 0, 0, 0, 0)
source_comp = (0, 1, 2, 0, 0, 0, 1, 1, 1, 2, 2, 2, 0, 1, 2, 1)
target_comp = (0, 1, 2, 0, 0, 0, 1, 1, 1, 2, 2, 2, 1, 2, 0, 0)
TERMS = len(stencil_kind)
COMPONENTS = 3
MEMBERS = tuple(
    tuple(q for q in range(TERMS) if target_comp[q] == target) for target in range(COMPONENTS)
)
ORDER = tuple(q for members in MEMBERS for q in members)
M = 256
R = 64
NY = 8
NZ = 128
CELLS = NY * NZ
SNAP = 4
COLS = M // SNAP
OWN = R // SNAP
SPACE = ("z", "y", "core")
PIECES = 4
LIMIT = 24 * 1024 * 1024
WHOLE = 60 * 1024 * 1024


def mode_weight(factor, singular):
    return (factor / jnp.sqrt(singular)[None, :]).astype(jnp.bfloat16)


TILES = 8
GROUP = NZ // SNAP
WEIGHT_AT = COMPONENTS * TILES
COEFF_AT = WEIGHT_AT + 2
HELD = COEFF_AT + 2


def spread_rows(layer, out_ref, first, at):
    rows = jnp.swapaxes(layer, 0, 1)
    for half in range(2):
        group = [rows[half * 4 + i] for i in range(4)]
        for quarter in range(SNAP):
            lanes = slice(quarter * GROUP, (quarter + 1) * GROUP)
            out_ref[quarter, first + half, at : at + layer.shape[0]] = jnp.concatenate(
                [row[:, lanes] for row in group], axis=1
            )


def direct_kernel(snaps_ref, out_ref, raw, spread, arrived, sent):
    count = COLS // PIECES
    parts = [pl.ds(n * count, count) for n in range(PIECES)]
    arrivals = [
        pltpu.make_async_copy(snaps_ref.at[part], raw.at[part], arrived.at[n])
        for n, part in enumerate(parts)
    ]
    for copy in arrivals:
        copy.start()
    departures = []
    for n, part in enumerate(parts):
        arrivals[n].wait()
        for comp in range(COMPONENTS):
            for x in range(4):
                spread_rows(raw[part, comp, x], spread, comp * TILES + x * 2, n * count)
        departures.append(
            pltpu.make_async_copy(spread.at[:, :, part], out_ref.at[:, :, part], sent.at[n])
        )
        departures[-1].start()
    for copy in departures:
        copy.wait()


def adjoint_kernel(
    snap_ref,
    snaps_ref,
    left_ref,
    right_ref,
    coeff_ref,
    selector_ref,
    own_ref,
    next_ref,
    far_ref,
    previous_ref,
    left_out,
    right_out,
    coeff_out,
    selector_out,
    spread,
):
    for comp in range(COMPONENTS):
        for x in range(4):
            spread_rows(snaps_ref[:, comp, x], spread, comp * TILES + x * 2, 0)
    for n, ref in enumerate((own_ref, next_ref, far_ref, previous_ref)):
        ref[...] = spread[lax.rem(snap_ref[0] + n, SNAP)]
    left_out[...] = left_ref[...]
    right_out[...] = right_ref[...]
    selector_out[...] = selector_ref[...]
    shift = lax.rem(NZ - GROUP * snap_ref[0], NZ)
    for q in range(TERMS):
        for x in range(4):
            own = pltpu.roll(coeff_ref[q, x], shift, 1)
            for half in range(2):
                row = q * TILES + x * 2 + half
                coeff_out[row : row + 1, :] = jnp.concatenate(
                    [own[half * 4 + i : half * 4 + i + 1, :GROUP] for i in range(4)], axis=1
                )


def columns(refs, comp, tiles):
    return jnp.concatenate(
        [
            jnp.concatenate([ref[comp * TILES + t] for ref in refs], axis=0)
            for t in tiles
        ],
        axis=1,
    )


def modes_kernel(
    snaps_ref,
    weight_ref,
    adjoint_weight_ref,
    coeff_ref,
    held_ref,
    first_ref,
    last_ref,
    low_ref,
    high_ref,
):
    for n in range(2):
        wide = adjoint_weight_ref[:, n * NZ : (n + 1) * NZ].astype(jnp.float32)
        held_ref[WEIGHT_AT + n] = wide
        held_ref[COEFF_AT + n] = coeff_ref[n * R : (n + 1) * R, :]
    weight = weight_ref[...]
    blocks = [snaps_ref.at[n] for n in range(SNAP)]
    place = lax.rem(lax.broadcasted_iota(jnp.int32, (R, NZ), 1), GROUP)
    low = jnp.zeros((R, NZ), jnp.float32)
    high = jnp.zeros((R, NZ), jnp.float32)
    for comp in range(COMPONENTS):
        for t in range(0, TILES, 2):
            block = columns(blocks, comp, (t, t + 1))
            modes = jnp.dot(weight, block, preferred_element_type=jnp.float32)
            modes = modes.astype(jnp.bfloat16)
            for half in range(2):
                tile = modes[:, half * NZ : (half + 1) * NZ]
                index = comp * TILES + t + half
                wide = tile.astype(jnp.float32)
                held_ref[index] = wide
                if t == 0:
                    first_ref[comp * 2 + half] = tile
                if t == TILES - 2:
                    last_ref[comp * 2 + half] = tile
                edge = jnp.where(place == 0, wide, 0.0)
                low = low + (pltpu.roll(edge, index, 1) if index else edge)
                edge = jnp.where(place == GROUP - 1, wide, 0.0)
                high = high + pltpu.roll(edge, NZ + index - (GROUP - 1), 1)
    low_ref[...] = low.astype(jnp.bfloat16)
    high_ref[...] = high.astype(jnp.bfloat16)


def weighted_terms(comp, held_ref, before, after, below, above, out_ref):
    lane = lax.broadcasted_iota(jnp.int32, (R, NZ), 1)
    place = lax.rem(lane, GROUP)
    base = [0]
    for members in MEMBERS:
        base.append(base[-1] + len(members) * R)

    def put(q, t, value):
        target = target_comp[q]
        count = len(MEMBERS[target])
        at = MEMBERS[target].index(q)
        row = (q * TILES + t) % R
        coeff = held_ref[COEFF_AT + q * TILES // R, row : row + 1, :]
        value = (value * coeff).astype(jnp.bfloat16)
        for block in range(SNAP):
            row = base[target] + (block * count + at) * OWN
            out_ref[row : row + OWN, t * NZ : (t + 1) * NZ] = value[block * OWN : (block + 1) * OWN]

    field = [held_ref[comp * TILES + t] for t in range(TILES)]
    down = before[comp * 2 : comp * 2 + 2] + field[:-2]
    up = field[2:] + after[comp * 2 : comp * 2 + 2]
    for x in range(4):
        pair = field[2 * x : 2 * x + 2]
        ahead = [pltpu.roll(v, NZ - GROUP, 1) for v in pair]
        behind = [pltpu.roll(v, GROUP, 1) for v in pair]
        for half in range(2):
            t = 2 * x + half
            index = comp * TILES + t
            center = pair[half]
            x_up, x_down = up[t], down[t]
            y_up = jnp.where(lane >= NZ - GROUP, ahead[1] if half == 0 else 0.0, ahead[half])
            y_down = jnp.where(lane < GROUP, behind[0] if half == 1 else 0.0, behind[half])
            z_up = jnp.where(
                place == GROUP - 1,
                pltpu.roll(above, GROUP - 1 - index, 1),
                pltpu.roll(center, NZ - 1, 1),
            )
            z_down = jnp.where(
                place == 0,
                pltpu.roll(below, NZ - index, 1) if index else below,
                pltpu.roll(center, 1, 1),
            )
            for q in range(TERMS):
                if source_comp[q] != comp:
                    continue
                kind = stencil_kind[q]
                if kind == 0:
                    value = center
                elif kind == 1:
                    value = 0.5 * (x_up - x_down)
                elif kind == 2:
                    value = 0.5 * (y_up - y_down)
                elif kind == 3:
                    value = 0.5 * (z_up - z_down)
                else:
                    beside = x_up + x_down
                    beside = beside + y_up + y_down
                    beside = beside + z_up + z_down
                    value = beside - 6.0 * center
                put(q, t, value)


def products_kernel(
    scale,
    own_ref,
    next_ref,
    far_ref,
    previous_ref,
    direct_ref,
    held_hbm,
    before_ref,
    after_ref,
    below_ref,
    above_ref,
    keep_ref,
    send_ref,
    held_ref,
    gram_ref,
    parts_ref,
    weighted_ref,
    out_ref,
    sem,
):
    fetch = pltpu.make_async_copy(held_hbm, held_ref, sem)
    fetch.start()
    adjoints = (own_ref, next_ref, far_ref, previous_ref)
    directs = [direct_ref.at[n] for n in range(SNAP)]
    here = lax.axis_index("snap")
    transposed = (((1,), (1,)), ((), ()))
    gram = jnp.zeros((M, M), jnp.float32)
    for comp in range(COMPONENTS):
        for t in range(0, TILES, 2):
            gram = gram + lax.dot_general(
                columns(directs, comp, (t, t + 1)),
                columns(adjoints, comp, (t, t + 1)),
                transposed,
                preferred_element_type=jnp.float32,
            )
    fetch.wait()
    below = below_ref[...].astype(jnp.float32)
    above = above_ref[...].astype(jnp.float32)
    before = [before_ref[n].astype(jnp.float32) for n in range(6)]
    after = [after_ref[n].astype(jnp.float32) for n in range(6)]
    weight = jnp.concatenate([held_ref[WEIGHT_AT], held_ref[WEIGHT_AT + 1]], axis=1)
    weight = weight.astype(jnp.bfloat16)
    for comp in range(COMPONENTS):
        for t in range(0, TILES, 2):
            adjoint = columns(adjoints, comp, (t, t + 1))
            modes = jnp.dot(weight, adjoint, preferred_element_type=jnp.float32)
            high = modes.astype(jnp.bfloat16)
            rest = modes - high.astype(jnp.float32)
            middle = rest.astype(jnp.bfloat16)
            low = (rest - middle.astype(jnp.float32)).astype(jnp.bfloat16)
            for part, value in enumerate((high, middle, low)):
                parts_ref[comp, part * R : (part + 1) * R, t * NZ : (t + 2) * NZ] = value
        weighted_terms(comp, held_ref, before, after, below, above, weighted_ref)
    gram = gram * scale
    gram_ref[0] = gram[:, :NZ]
    gram_ref[1] = gram[:, NZ:]
    for core in range(2):
        for snap in range(SNAP):
            half, at = snap // 2, (snap % 2) * COLS
            halves = [
                gram_ref[half, pl.ds(2 * core + t, M // 4, stride=4), :][:, at : at + COLS]
                for t in range(2)
            ]
            chunk = core * SNAP + lax.rem(here + snap, SNAP)
            out_ref[chunk, :64, :] = jnp.concatenate(halves, axis=1)
    blocks = []
    row = 0
    for target, members in enumerate(MEMBERS):
        count = len(members) * R
        product = lax.dot_general(
            parts_ref[target],
            weighted_ref[row : row + count, :],
            transposed,
            preferred_element_type=jnp.float32,
        )
        row += count
        blocks.append((product[:R] + (product[R : 2 * R] + product[2 * R :])) * scale)
    for snap in range(SNAP):
        own = jnp.concatenate(
            [
                block[:, snap * (block.shape[1] // SNAP) : (snap + 1) * (block.shape[1] // SNAP)]
                for block in blocks
            ],
            axis=1,
        )
        for core in range(2):
            for w in range(4):
                rows = own[(2 * w + core) * 8 : (2 * w + core + 1) * 8]
                out_ref[core * SNAP + snap, 64 + w * 8 : 64 + w * 8 + 8, :] = rows[:, :NZ]
                out_ref[core * SNAP + snap, 96 + w * 8 : 96 + w * 8 + 8, :] = rows[:, NZ:]
    core = lax.axis_index("core")
    keep_ref[...] = out_ref[pl.ds(core * SNAP, SNAP)]
    send_ref[...] = out_ref[pl.ds((1 - core) * SNAP, SNAP)]


def finish_kernel(sums_ref, gram_ref, reduced_ref):
    total = jnp.sum(sums_ref[...], axis=0)
    gram_ref[...] = jnp.concatenate([total[0:1, :COLS], total[0:1, COLS:]], axis=0)
    reduced_ref[...] = jnp.concatenate(
        [total[1:2, v * OWN : (v + 1) * OWN] for v in range(8)], axis=0
    )


def call(kernel, out_shape, flops, moved, scratch=(), inputs=None, outputs=None, limit=LIMIT):
    def run(*operands):
        spaces = dict.fromkeys(range(len(operands)), pltpu.VMEM) | (inputs or {})
        results = pl.BlockSpec(memory_space=outputs or pltpu.VMEM)
        several = isinstance(out_shape, tuple)
        return pl.pallas_call(
            kernel,
            out_shape=out_shape,
            in_specs=[pl.BlockSpec(memory_space=space) for space in spaces.values()],
            out_specs=[results] * len(out_shape) if several else results,
            scratch_shapes=list(scratch),
            compiler_params=pltpu.CompilerParams(vmem_limit_bytes=limit),
            cost_estimate=pl.CostEstimate(flops=flops, bytes_accessed=moved, transcendentals=0),
        )(*operands)

    return run


def shards(direct_snaps, adjoint_snaps, left_factor, right_factor, singular, term_coeff, term_slot):
    scale = 1.0 / math.sqrt(1572864)
    turned = jnp.roll(left_factor, -COLS * lax.axis_index("snap"), axis=0)
    left = mode_weight(turned, singular).T
    right = mode_weight(right_factor, singular).T
    tiles = COMPONENTS * TILES

    def shape(*dims, dtype=jnp.bfloat16):
        return jax.ShapeDtypeStruct(dims, dtype)

    spread_shape = shape(SNAP, tiles, COLS, NZ)
    ready = call(
        direct_kernel,
        pltpu.HBM(spread_shape.shape, jnp.bfloat16),
        0,
        3 << 20,
        (
            pltpu.VMEM(direct_snaps.shape, jnp.bfloat16),
            pltpu.VMEM((SNAP, tiles, COLS, NZ), jnp.bfloat16),
            pltpu.SemaphoreType.DMA((PIECES,)),
            pltpu.SemaphoreType.DMA((PIECES,)),
        ),
        {0: pl.ANY},
        pltpu.HBM,
        WHOLE,
    )(direct_snaps)
    direct = lax.all_to_all(ready, "snap", 0, 0, tiled=True)
    selector = (
        term_slot[jnp.array(ORDER)][None, :] == jnp.arange(TERMS, dtype=jnp.int32)[:, None]
    ).astype(jnp.float32)
    here = lax.axis_index("snap").astype(jnp.int32).reshape(1)
    own, *others, adjoint_weight, direct_weight, coeff, selector = call(
        adjoint_kernel,
        (
            *[shape(tiles, COLS, NZ)] * SNAP,
            pltpu.HBM((R, M), jnp.bfloat16),
            pltpu.HBM((R, M), jnp.bfloat16),
            pltpu.HBM((TERMS * TILES, NZ), jnp.float32),
            pltpu.HBM((TERMS, TERMS), jnp.float32),
        ),
        0,
        3 << 20,
        (pltpu.VMEM((SNAP, tiles, COLS, NZ), jnp.bfloat16),),
        {0: pltpu.SMEM},
    )(here, adjoint_snaps, left, right, term_coeff, selector)
    arrived = [
        lax.ppermute(piece, "snap", [(i, (i + n) % SNAP) for i in range(SNAP)])
        for n, piece in enumerate(others, 1)
    ]
    adjoints = (own, *arrived[::-1])
    held, first, last, low, high = call(
        modes_kernel,
        (
            pltpu.HBM((HELD, R, NZ), jnp.float32),
            shape(6, R, NZ),
            shape(6, R, NZ),
            shape(R, NZ),
            shape(R, NZ),
        ),
        2 * R * M * 3 * CELLS,
        2 << 20,
    )(direct, direct_weight, adjoint_weight, coeff)
    held = pltpu.with_memory_space_constraint(held, pltpu.HBM)
    slabs, quarters = ([(i, i + 1) for i in range(n - 1)] for n in (128, SNAP))
    before = lax.ppermute(last, SPACE, slabs)
    after = lax.ppermute(first, SPACE, [(j, i) for i, j in slabs])
    below = lax.ppermute(high, "snap", quarters)
    above = lax.ppermute(low, "snap", [(j, i) for i, j in quarters])
    half = shape(SNAP, 128, NZ, dtype=jnp.float32)
    keep, send = call(
        functools.partial(products_kernel, scale),
        (half, half),
        1 << 30,
        6 << 20,
        (
            pltpu.VMEM((HELD, R, NZ), jnp.float32),
            pltpu.VMEM((2, M, NZ), jnp.float32),
            pltpu.VMEM((COMPONENTS, 3 * R, CELLS), jnp.bfloat16),
            pltpu.VMEM((TERMS * R, CELLS), jnp.bfloat16),
            pltpu.VMEM((2 * SNAP, 128, NZ), jnp.float32),
            pltpu.SemaphoreType.DMA,
        ),
        {5: pltpu.HBM},
    )(*adjoints, direct, held, before, after, below, above)
    terms = keep + lax.ppermute(send, "core", [(0, 1), (1, 0)])
    near = lax.all_to_all(terms, "snap", 0, 0, tiled=True).sum(axis=0)
    gram = near[:64]
    operators = near[64:].reshape(2, 4, 8, 8, OWN).transpose(0, 3, 1, 2, 4).reshape(TERMS, 4 * NZ)
    ordered = jnp.dot(selector, operators, precision=lax.Precision.HIGHEST)
    owned = jnp.stack([gram, ordered.reshape(64, NZ)], axis=1)
    sums = lax.all_to_all(owned, ("z", "y"), 0, 0, tiled=True)
    outs = (shape(2, COLS, dtype=jnp.float32), shape(8, OWN, dtype=jnp.float32))
    gram, reduced = call(finish_kernel, outs, 0, 1 << 16)(sums)
    return (gram.T, reduced)


def solution(mesh):
    parts = Mesh(mesh.devices.reshape(8, 8, 2, 4), SPACE + ("snap",))
    return jax.shard_map(
        shards,
        mesh=parts,
        in_specs=(
            P("snap", None, SPACE, None, None),
            P("snap", None, SPACE, None, None),
            P(),
            P(),
            P(),
            P(None, SPACE, None, None),
            P(),
        ),
        out_specs=(P("snap", SPACE), P(SPACE, "snap")),
        check_vma=False,
    )
```

```python
import functools
import math

import jax
import jax.numpy as jnp
from jax import lax
from jax.experimental import pallas as pl
from jax.experimental.pallas import tpu as pltpu
from jax.sharding import Mesh, PartitionSpec as P

stencil_kind = (4, 4, 4, 1, 2, 3, 1, 2, 3, 1, 2, 3, 0, 0, 0, 0)
source_comp = (0, 1, 2, 0, 0, 0, 1, 1, 1, 2, 2, 2, 0, 1, 2, 1)
target_comp = (0, 1, 2, 0, 0, 0, 1, 1, 1, 2, 2, 2, 1, 2, 0, 0)
TERMS = len(stencil_kind)
COMPONENTS = 3
MEMBERS = tuple(
    tuple(q for q in range(TERMS) if target_comp[q] == target) for target in range(COMPONENTS)
)
ORDER = tuple(q for members in MEMBERS for q in members)
M = 256
R = 64
NY = 8
NZ = 128
CELLS = NY * NZ
SNAP = 4
COLS = M // SNAP
OWN = R // SNAP
SPACE = ("z", "y", "core")
PIECES = 4
LIMIT = 24 * 1024 * 1024
WHOLE = 60 * 1024 * 1024


def mode_weight(factor, singular):
    return (factor / jnp.sqrt(singular)[None, :]).astype(jnp.bfloat16)


TILES = 8
GROUP = NZ // SNAP
WEIGHT_AT = COMPONENTS * TILES
COEFF_AT = WEIGHT_AT + 2
TURNED_AT = COEFF_AT + 2
HELD = TURNED_AT + 2
SENT = COMPONENTS * TILES + 2


def spread_rows(layer, out_ref, first, at):
    rows = jnp.swapaxes(layer, 0, 1)
    for half in range(2):
        group = [rows[half * 4 + i] for i in range(4)]
        for quarter in range(SNAP):
            lanes = slice(quarter * GROUP, (quarter + 1) * GROUP)
            out_ref[quarter, first + half, at : at + layer.shape[0]] = jnp.concatenate(
                [row[:, lanes] for row in group], axis=1
            )


def direct_kernel(snaps_ref, out_ref, raw, spread, arrived, sent):
    count = COLS // PIECES
    parts = [pl.ds(n * count, count) for n in range(PIECES)]
    arrivals = [
        pltpu.make_async_copy(snaps_ref.at[part], raw.at[part], arrived.at[n])
        for n, part in enumerate(parts)
    ]
    for copy in arrivals:
        copy.start()
    departures = []
    for n, part in enumerate(parts):
        arrivals[n].wait()
        for comp in range(COMPONENTS):
            for x in range(4):
                spread_rows(raw[part, comp, x], spread, comp * TILES + x * 2, n * count)
        departures.append(
            pltpu.make_async_copy(spread.at[:, :, part], out_ref.at[:, :, part], sent.at[n])
        )
        departures[-1].start()
    for copy in departures:
        copy.wait()


def adjoint_kernel(
    snap_ref,
    snaps_ref,
    left_ref,
    right_ref,
    turned_ref,
    coeff_ref,
    selector_ref,
    ready_ref,
    own_ref,
    next_ref,
    far_ref,
    previous_ref,
    left_out,
    right_out,
    turned_out,
    coeff_out,
    selector_out,
    spread,
):
    for comp in range(COMPONENTS):
        for x in range(4):
            spread_rows(snaps_ref[:, comp, x], spread, comp * TILES + x * 2, 0)
    place = lax.rem(lax.broadcasted_iota(jnp.int32, (COLS, NZ), 1), GROUP)
    empty = jnp.zeros((COLS, NZ), jnp.bfloat16)
    spread[0, SENT - 2] = empty
    spread[SNAP - 1, SENT - 1] = empty
    for quarter in range(SNAP):
        low = jnp.zeros((COLS, NZ), jnp.float32)
        high = jnp.zeros((COLS, NZ), jnp.float32)
        for index in range(COMPONENTS * TILES):
            wide = ready_ref[quarter, index].astype(jnp.float32)
            if quarter > 0:
                edge = jnp.where(place == 0, wide, 0.0)
                low = low + (pltpu.roll(edge, index, 1) if index else edge)
            if quarter < SNAP - 1:
                edge = jnp.where(place == GROUP - 1, wide, 0.0)
                high = high + pltpu.roll(edge, NZ + index - (GROUP - 1), 1)
        if quarter > 0:
            spread[quarter - 1, SENT - 1] = low.astype(jnp.bfloat16)
        if quarter < SNAP - 1:
            spread[quarter + 1, SENT - 2] = high.astype(jnp.bfloat16)
    for n, ref in enumerate((own_ref, next_ref, far_ref, previous_ref)):
        ref[...] = spread[lax.rem(snap_ref[0] + n, SNAP)]
    left_out[...] = left_ref[...]
    right_out[...] = right_ref[...]
    turned_out[...] = turned_ref[...]
    selector_out[...] = selector_ref[...]
    shift = lax.rem(NZ - GROUP * snap_ref[0], NZ)
    for q in range(TERMS):
        for x in range(4):
            own = pltpu.roll(coeff_ref[q, x], shift, 1)
            for half in range(2):
                row = q * TILES + x * 2 + half
                coeff_out[row : row + 1, :] = jnp.concatenate(
                    [own[half * 4 + i : half * 4 + i + 1, :GROUP] for i in range(4)], axis=1
                )


def columns(refs, comp, tiles):
    return jnp.concatenate(
        [
            jnp.concatenate([ref[comp * TILES + t] for ref in refs], axis=0)
            for t in tiles
        ],
        axis=1,
    )


def modes_kernel(
    snaps_ref, weight_ref, adjoint_weight_ref, turned_ref, coeff_ref, held_ref, first_ref, last_ref
):
    for n in range(2):
        half = slice(n * NZ, (n + 1) * NZ)
        held_ref[WEIGHT_AT + n] = adjoint_weight_ref[:, half].astype(jnp.float32)
        held_ref[TURNED_AT + n] = turned_ref[:, half].astype(jnp.float32)
        held_ref[COEFF_AT + n] = coeff_ref[n * R : (n + 1) * R, :]
    weight = weight_ref[...]
    blocks = [snaps_ref.at[n] for n in range(SNAP)]
    for comp in range(COMPONENTS):
        for t in range(0, TILES, 2):
            block = columns(blocks, comp, (t, t + 1))
            modes = jnp.dot(weight, block, preferred_element_type=jnp.float32)
            modes = modes.astype(jnp.bfloat16)
            for half in range(2):
                tile = modes[:, half * NZ : (half + 1) * NZ]
                held_ref[comp * TILES + t + half] = tile.astype(jnp.float32)
                if t == 0:
                    first_ref[comp * 2 + half] = tile
                if t == TILES - 2:
                    last_ref[comp * 2 + half] = tile


def weighted_terms(comp, held_ref, before, after, below, above, out_ref):
    lane = lax.broadcasted_iota(jnp.int32, (R, NZ), 1)
    place = lax.rem(lane, GROUP)
    base = [0]
    for members in MEMBERS:
        base.append(base[-1] + len(members) * R)

    def put(q, t, value):
        target = target_comp[q]
        count = len(MEMBERS[target])
        at = MEMBERS[target].index(q)
        row = (q * TILES + t) % R
        coeff = held_ref[COEFF_AT + q * TILES // R, row : row + 1, :]
        value = (value * coeff).astype(jnp.bfloat16)
        for block in range(SNAP):
            row = base[target] + (block * count + at) * OWN
            out_ref[row : row + OWN, t * NZ : (t + 1) * NZ] = value[block * OWN : (block + 1) * OWN]

    field = [held_ref[comp * TILES + t] for t in range(TILES)]
    down = before[comp * 2 : comp * 2 + 2] + field[:-2]
    up = field[2:] + after[comp * 2 : comp * 2 + 2]
    for x in range(4):
        pair = field[2 * x : 2 * x + 2]
        ahead = [pltpu.roll(v, NZ - GROUP, 1) for v in pair]
        behind = [pltpu.roll(v, GROUP, 1) for v in pair]
        for half in range(2):
            t = 2 * x + half
            index = comp * TILES + t
            center = pair[half]
            x_up, x_down = up[t], down[t]
            y_up = jnp.where(lane >= NZ - GROUP, ahead[1] if half == 0 else 0.0, ahead[half])
            y_down = jnp.where(lane < GROUP, behind[0] if half == 1 else 0.0, behind[half])
            z_up = jnp.where(
                place == GROUP - 1,
                pltpu.roll(above, GROUP - 1 - index, 1),
                pltpu.roll(center, NZ - 1, 1),
            )
            z_down = jnp.where(
                place == 0,
                pltpu.roll(below, NZ - index, 1) if index else below,
                pltpu.roll(center, 1, 1),
            )
            for q in range(TERMS):
                if source_comp[q] != comp:
                    continue
                kind = stencil_kind[q]
                if kind == 0:
                    value = center
                elif kind == 1:
                    value = 0.5 * (x_up - x_down)
                elif kind == 2:
                    value = 0.5 * (y_up - y_down)
                elif kind == 3:
                    value = 0.5 * (z_up - z_down)
                else:
                    beside = x_up + x_down
                    beside = beside + y_up + y_down
                    beside = beside + z_up + z_down
                    value = beside - 6.0 * center
                put(q, t, value)


def products_kernel(
    scale,
    own_ref,
    next_ref,
    far_ref,
    previous_ref,
    direct_ref,
    held_hbm,
    before_ref,
    after_ref,
    keep_ref,
    send_ref,
    held_ref,
    gram_ref,
    parts_ref,
    weighted_ref,
    out_ref,
    sem,
):
    fetch = pltpu.make_async_copy(held_hbm, held_ref, sem)
    fetch.start()
    adjoints = (own_ref, next_ref, far_ref, previous_ref)
    directs = [direct_ref.at[n] for n in range(SNAP)]
    here = lax.axis_index("snap")
    transposed = (((1,), (1,)), ((), ()))
    gram = jnp.zeros((M, M), jnp.float32)
    for comp in range(COMPONENTS):
        for t in range(0, TILES, 2):
            gram = gram + lax.dot_general(
                columns(directs, comp, (t, t + 1)),
                columns(adjoints, comp, (t, t + 1)),
                transposed,
                preferred_element_type=jnp.float32,
            )
    fetch.wait()
    turned, weight = (
        jnp.concatenate([held_ref[at], held_ref[at + 1]], axis=1).astype(jnp.bfloat16)
        for at in (TURNED_AT, WEIGHT_AT)
    )
    edges = jnp.dot(turned, columns(adjoints, COMPONENTS, (0, 1)), preferred_element_type=jnp.float32)
    edges = edges.astype(jnp.bfloat16).astype(jnp.float32)
    below, above = edges[:, :NZ], edges[:, NZ:]
    before = [before_ref[n].astype(jnp.float32) for n in range(6)]
    after = [after_ref[n].astype(jnp.float32) for n in range(6)]
    for comp in range(COMPONENTS):
        for t in range(0, TILES, 2):
            adjoint = columns(adjoints, comp, (t, t + 1))
            modes = jnp.dot(weight, adjoint, preferred_element_type=jnp.float32)
            high = modes.astype(jnp.bfloat16)
            rest = modes - high.astype(jnp.float32)
            middle = rest.astype(jnp.bfloat16)
            low = (rest - middle.astype(jnp.float32)).astype(jnp.bfloat16)
            for part, value in enumerate((high, middle, low)):
                parts_ref[comp, part * R : (part + 1) * R, t * NZ : (t + 2) * NZ] = value
        weighted_terms(comp, held_ref, before, after, below, above, weighted_ref)
    gram = gram * scale
    gram_ref[0] = gram[:, :NZ]
    gram_ref[1] = gram[:, NZ:]
    for core in range(2):
        for snap in range(SNAP):
            half, at = snap // 2, (snap % 2) * COLS
            halves = [
                gram_ref[half, pl.ds(2 * core + t, M // 4, stride=4), :][:, at : at + COLS]
                for t in range(2)
            ]
            chunk = core * SNAP + lax.rem(here + snap, SNAP)
            out_ref[chunk, :64, :] = jnp.concatenate(halves, axis=1)
    blocks = []
    row = 0
    for target, members in enumerate(MEMBERS):
        count = len(members) * R
        product = lax.dot_general(
            parts_ref[target],
            weighted_ref[row : row + count, :],
            transposed,
            preferred_element_type=jnp.float32,
        )
        row += count
        blocks.append((product[:R] + (product[R : 2 * R] + product[2 * R :])) * scale)
    for snap in range(SNAP):
        own = jnp.concatenate(
            [
                block[:, snap * (block.shape[1] // SNAP) : (snap + 1) * (block.shape[1] // SNAP)]
                for block in blocks
            ],
            axis=1,
        )
        for core in range(2):
            for w in range(4):
                rows = own[(2 * w + core) * 8 : (2 * w + core + 1) * 8]
                out_ref[core * SNAP + snap, 64 + w * 8 : 64 + w * 8 + 8, :] = rows[:, :NZ]
                out_ref[core * SNAP + snap, 96 + w * 8 : 96 + w * 8 + 8, :] = rows[:, NZ:]
    core = lax.axis_index("core")
    keep_ref[...] = out_ref[pl.ds(core * SNAP, SNAP)]
    send_ref[...] = out_ref[pl.ds((1 - core) * SNAP, SNAP)]


def finish_kernel(sums_ref, gram_ref, reduced_ref):
    total = jnp.sum(sums_ref[...], axis=0)
    gram_ref[...] = jnp.concatenate([total[0:1, :COLS], total[0:1, COLS:]], axis=0)
    reduced_ref[...] = jnp.concatenate(
        [total[1:2, v * OWN : (v + 1) * OWN] for v in range(8)], axis=0
    )


def call(kernel, out_shape, flops, moved, scratch=(), inputs=None, outputs=None, limit=LIMIT):
    def run(*operands):
        spaces = dict.fromkeys(range(len(operands)), pltpu.VMEM) | (inputs or {})
        results = pl.BlockSpec(memory_space=outputs or pltpu.VMEM)
        several = isinstance(out_shape, tuple)
        return pl.pallas_call(
            kernel,
            out_shape=out_shape,
            in_specs=[pl.BlockSpec(memory_space=space) for space in spaces.values()],
            out_specs=[results] * len(out_shape) if several else results,
            scratch_shapes=list(scratch),
            compiler_params=pltpu.CompilerParams(vmem_limit_bytes=limit),
            cost_estimate=pl.CostEstimate(flops=flops, bytes_accessed=moved, transcendentals=0),
        )(*operands)

    return run


def shards(direct_snaps, adjoint_snaps, left_factor, right_factor, singular, term_coeff, term_slot):
    scale = 1.0 / math.sqrt(1572864)
    back = -COLS * lax.axis_index("snap")
    left = mode_weight(jnp.roll(left_factor, back, axis=0), singular).T
    right = mode_weight(right_factor, singular).T
    turned = jnp.roll(right, back, axis=1)
    tiles = COMPONENTS * TILES

    def shape(*dims, dtype=jnp.bfloat16):
        return jax.ShapeDtypeStruct(dims, dtype)

    spread_shape = shape(SNAP, tiles, COLS, NZ)
    ready = call(
        direct_kernel,
        pltpu.HBM(spread_shape.shape, jnp.bfloat16),
        0,
        3 << 20,
        (
            pltpu.VMEM(direct_snaps.shape, jnp.bfloat16),
            pltpu.VMEM((SNAP, tiles, COLS, NZ), jnp.bfloat16),
            pltpu.SemaphoreType.DMA((PIECES,)),
            pltpu.SemaphoreType.DMA((PIECES,)),
        ),
        {0: pl.ANY},
        pltpu.HBM,
        WHOLE,
    )(direct_snaps)
    direct = lax.all_to_all(ready, "snap", 0, 0, tiled=True)
    selector = (
        term_slot[jnp.array(ORDER)][None, :] == jnp.arange(TERMS, dtype=jnp.int32)[:, None]
    ).astype(jnp.float32)
    here = lax.axis_index("snap").astype(jnp.int32).reshape(1)
    own, *others, adjoint_weight, direct_weight, turned, coeff, selector = call(
        adjoint_kernel,
        (
            *[shape(SENT, COLS, NZ)] * SNAP,
            pltpu.HBM((R, M), jnp.bfloat16),
            pltpu.HBM((R, M), jnp.bfloat16),
            pltpu.HBM((R, M), jnp.bfloat16),
            pltpu.HBM((TERMS * TILES, NZ), jnp.float32),
            pltpu.HBM((TERMS, TERMS), jnp.float32),
        ),
        0,
        3 << 20,
        (pltpu.VMEM((SNAP, SENT, COLS, NZ), jnp.bfloat16),),
        {0: pltpu.SMEM},
    )(here, adjoint_snaps, left, right, turned, term_coeff, selector, ready)
    arrived = [
        lax.ppermute(piece, "snap", [(i, (i + n) % SNAP) for i in range(SNAP)])
        for n, piece in enumerate(others, 1)
    ]
    adjoints = (own, *arrived[::-1])
    held, first, last = call(
        modes_kernel,
        (pltpu.HBM((HELD, R, NZ), jnp.float32), shape(6, R, NZ), shape(6, R, NZ)),
        2 * R * M * 3 * CELLS,
        2 << 20,
    )(direct, direct_weight, adjoint_weight, turned, coeff)
    held = pltpu.with_memory_space_constraint(held, pltpu.HBM)
    slabs = [(i, i + 1) for i in range(127)]
    before = lax.ppermute(last, SPACE, slabs)
    after = lax.ppermute(first, SPACE, [(j, i) for i, j in slabs])
    half = shape(SNAP, 128, NZ, dtype=jnp.float32)
    keep, send = call(
        functools.partial(products_kernel, scale),
        (half, half),
        1 << 30,
        6 << 20,
        (
            pltpu.VMEM((HELD, R, NZ), jnp.float32),
            pltpu.VMEM((2, M, NZ), jnp.float32),
            pltpu.VMEM((COMPONENTS, 3 * R, CELLS), jnp.bfloat16),
            pltpu.VMEM((TERMS * R, CELLS), jnp.bfloat16),
            pltpu.VMEM((2 * SNAP, 128, NZ), jnp.float32),
            pltpu.SemaphoreType.DMA,
        ),
        {5: pltpu.HBM},
    )(*adjoints, direct, held, before, after)
    terms = keep + lax.ppermute(send, "core", [(0, 1), (1, 0)])
    near = lax.all_to_all(terms, "snap", 0, 0, tiled=True).sum(axis=0)
    gram = near[:64]
    operators = near[64:].reshape(2, 4, 8, 8, OWN).transpose(0, 3, 1, 2, 4).reshape(TERMS, 4 * NZ)
    ordered = jnp.dot(selector, operators, precision=lax.Precision.HIGHEST)
    owned = jnp.stack([gram, ordered.reshape(64, NZ)], axis=1)
    sums = lax.all_to_all(owned, ("z", "y"), 0, 0, tiled=True)
    outs = (shape(2, COLS, dtype=jnp.float32), shape(8, OWN, dtype=jnp.float32))
    gram, reduced = call(finish_kernel, outs, 0, 1 << 16)(sums)
    return (gram.T, reduced)


def solution(mesh):
    parts = Mesh(mesh.devices.reshape(8, 8, 2, 4), SPACE + ("snap",))
    return jax.shard_map(
        shards,
        mesh=parts,
        in_specs=(
            P("snap", None, SPACE, None, None),
            P("snap", None, SPACE, None, None),
            P(),
            P(),
            P(),
            P(None, SPACE, None, None),
            P(),
        ),
        out_specs=(P("snap", SPACE), P(SPACE, "snap")),
        check_vma=False,
    )
```

```python
import functools
import math

import jax
import jax.numpy as jnp
from jax import lax
from jax.experimental import pallas as pl
from jax.experimental.pallas import tpu as pltpu
from jax.sharding import Mesh, PartitionSpec as P

stencil_kind = (4, 4, 4, 1, 2, 3, 1, 2, 3, 1, 2, 3, 0, 0, 0, 0)
source_comp = (0, 1, 2, 0, 0, 0, 1, 1, 1, 2, 2, 2, 0, 1, 2, 1)
target_comp = (0, 1, 2, 0, 0, 0, 1, 1, 1, 2, 2, 2, 1, 2, 0, 0)
TERMS = len(stencil_kind)
COMPONENTS = 3
MEMBERS = tuple(
    tuple(q for q in range(TERMS) if target_comp[q] == target) for target in range(COMPONENTS)
)
ORDER = tuple(q for members in MEMBERS for q in members)
M = 256
R = 64
NY = 8
NZ = 128
CELLS = NY * NZ
SNAP = 4
COLS = M // SNAP
OWN = R // SNAP
SPACE = ("z", "y", "core")
PIECES = 4
LIMIT = 24 * 1024 * 1024
WHOLE = 60 * 1024 * 1024


def mode_weight(factor, singular):
    return (factor / jnp.sqrt(singular)[None, :]).astype(jnp.bfloat16)


TILES = 8
GROUP = NZ // SNAP
WEIGHT_AT = 0
COEFF_AT = WEIGHT_AT + 2
TURNED_AT = COEFF_AT + 2
EXTRAS = TURNED_AT + 2
SENT = COMPONENTS * TILES + 2


def spread_rows(layer, out_ref, first, at):
    rows = jnp.swapaxes(layer, 0, 1)
    for half in range(2):
        group = [rows[half * 4 + i] for i in range(4)]
        for quarter in range(SNAP):
            lanes = slice(quarter * GROUP, (quarter + 1) * GROUP)
            out_ref[quarter, first + half, at : at + layer.shape[0]] = jnp.concatenate(
                [row[:, lanes] for row in group], axis=1
            )


def direct_kernel(snaps_ref, out_ref, raw, spread, arrived, sent):
    count = COLS // PIECES
    parts = [pl.ds(n * count, count) for n in range(PIECES)]
    arrivals = [
        pltpu.make_async_copy(snaps_ref.at[part], raw.at[part], arrived.at[n])
        for n, part in enumerate(parts)
    ]
    for copy in arrivals:
        copy.start()
    departures = []
    for n, part in enumerate(parts):
        arrivals[n].wait()
        for comp in range(COMPONENTS):
            for x in range(4):
                spread_rows(raw[part, comp, x], spread, comp * TILES + x * 2, n * count)
        departures.append(
            pltpu.make_async_copy(spread.at[:, :, part], out_ref.at[:, :, part], sent.at[n])
        )
        departures[-1].start()
    for copy in departures:
        copy.wait()


def adjoint_kernel(
    snap_ref,
    snaps_ref,
    ready_ref,
    weight_ref,
    own_ref,
    next_ref,
    far_ref,
    previous_ref,
    weight_out,
    spread,
):
    weight_out[...] = weight_ref[...]
    for comp in range(COMPONENTS):
        for x in range(4):
            spread_rows(snaps_ref[:, comp, x], spread, comp * TILES + x * 2, 0)
    place = lax.rem(lax.broadcasted_iota(jnp.int32, (COLS, NZ), 1), GROUP)
    empty = jnp.zeros((COLS, NZ), jnp.bfloat16)
    spread[0, SENT - 2] = empty
    spread[SNAP - 1, SENT - 1] = empty
    for quarter in range(SNAP):
        low = jnp.zeros((COLS, NZ), jnp.float32)
        high = jnp.zeros((COLS, NZ), jnp.float32)
        for index in range(COMPONENTS * TILES):
            wide = ready_ref[quarter, index].astype(jnp.float32)
            if quarter > 0:
                edge = jnp.where(place == 0, wide, 0.0)
                low = low + (pltpu.roll(edge, index, 1) if index else edge)
            if quarter < SNAP - 1:
                edge = jnp.where(place == GROUP - 1, wide, 0.0)
                high = high + pltpu.roll(edge, NZ + index - (GROUP - 1), 1)
        if quarter > 0:
            spread[quarter - 1, SENT - 1] = low.astype(jnp.bfloat16)
        if quarter < SNAP - 1:
            spread[quarter + 1, SENT - 2] = high.astype(jnp.bfloat16)
    for n, ref in enumerate((own_ref, next_ref, far_ref, previous_ref)):
        ref[...] = spread[lax.rem(snap_ref[0] + n, SNAP)]


def extras_kernel(snap_ref, left_ref, turned_ref, coeff_ref, selector_ref, _, out_ref, selector_out):
    selector_out[...] = selector_ref[...]
    for n in range(2):
        half = slice(n * NZ, (n + 1) * NZ)
        out_ref[WEIGHT_AT + n] = left_ref[:, half].astype(jnp.float32)
        out_ref[TURNED_AT + n] = turned_ref[:, half].astype(jnp.float32)
    shift = lax.rem(NZ - GROUP * snap_ref[0], NZ)
    for q in range(TERMS):
        for x in range(4):
            own = pltpu.roll(coeff_ref[q, x], shift, 1)
            for half in range(2):
                row = q * TILES + x * 2 + half
                out_ref[COEFF_AT + row // R, row % R : row % R + 1, :] = jnp.concatenate(
                    [own[half * 4 + i : half * 4 + i + 1, :GROUP] for i in range(4)], axis=1
                )


def columns(refs, comp, tiles):
    return jnp.concatenate(
        [
            jnp.concatenate([ref[comp * TILES + t] for ref in refs], axis=0)
            for t in tiles
        ],
        axis=1,
    )


def modes_kernel(snaps_ref, weight_ref, out_ref, first_ref, last_ref):
    weight = weight_ref[...]
    blocks = [snaps_ref.at[n] for n in range(SNAP)]
    for comp in range(COMPONENTS):
        for t in range(0, TILES, 2):
            block = columns(blocks, comp, (t, t + 1))
            modes = jnp.dot(weight, block, preferred_element_type=jnp.float32)
            modes = modes.astype(jnp.bfloat16)
            for half in range(2):
                tile = modes[:, half * NZ : (half + 1) * NZ]
                out_ref[comp * TILES + t + half] = tile.astype(jnp.float32)
                if t == 0:
                    first_ref[comp * 2 + half] = tile
                if t == TILES - 2:
                    last_ref[comp * 2 + half] = tile


def weighted_terms(comp, modes_ref, extras_ref, before, after, below, above, out_ref):
    lane = lax.broadcasted_iota(jnp.int32, (R, NZ), 1)
    place = lax.rem(lane, GROUP)
    base = [0]
    for members in MEMBERS:
        base.append(base[-1] + len(members) * R)

    def put(q, t, value):
        target = target_comp[q]
        count = len(MEMBERS[target])
        at = MEMBERS[target].index(q)
        row = (q * TILES + t) % R
        coeff = extras_ref[COEFF_AT + q * TILES // R, row : row + 1, :]
        value = (value * coeff).astype(jnp.bfloat16)
        for block in range(SNAP):
            row = base[target] + (block * count + at) * OWN
            out_ref[row : row + OWN, t * NZ : (t + 1) * NZ] = value[block * OWN : (block + 1) * OWN]

    field = [modes_ref[comp * TILES + t] for t in range(TILES)]
    down = before[comp * 2 : comp * 2 + 2] + field[:-2]
    up = field[2:] + after[comp * 2 : comp * 2 + 2]
    for x in range(4):
        pair = field[2 * x : 2 * x + 2]
        ahead = [pltpu.roll(v, NZ - GROUP, 1) for v in pair]
        behind = [pltpu.roll(v, GROUP, 1) for v in pair]
        for half in range(2):
            t = 2 * x + half
            index = comp * TILES + t
            center = pair[half]
            x_up, x_down = up[t], down[t]
            y_up = jnp.where(lane >= NZ - GROUP, ahead[1] if half == 0 else 0.0, ahead[half])
            y_down = jnp.where(lane < GROUP, behind[0] if half == 1 else 0.0, behind[half])
            z_up = jnp.where(
                place == GROUP - 1,
                pltpu.roll(above, GROUP - 1 - index, 1),
                pltpu.roll(center, NZ - 1, 1),
            )
            z_down = jnp.where(
                place == 0,
                pltpu.roll(below, NZ - index, 1) if index else below,
                pltpu.roll(center, 1, 1),
            )
            for q in range(TERMS):
                if source_comp[q] != comp:
                    continue
                kind = stencil_kind[q]
                if kind == 0:
                    value = center
                elif kind == 1:
                    value = 0.5 * (x_up - x_down)
                elif kind == 2:
                    value = 0.5 * (y_up - y_down)
                elif kind == 3:
                    value = 0.5 * (z_up - z_down)
                else:
                    beside = x_up + x_down
                    beside = beside + y_up + y_down
                    beside = beside + z_up + z_down
                    value = beside - 6.0 * center
                put(q, t, value)


def products_kernel(
    scale,
    own_ref,
    next_ref,
    far_ref,
    previous_ref,
    direct_ref,
    modes_hbm,
    extras_hbm,
    before_ref,
    after_ref,
    keep_ref,
    send_ref,
    modes_ref,
    extras_ref,
    gram_ref,
    parts_ref,
    weighted_ref,
    out_ref,
    sems,
):
    fetches = [
        pltpu.make_async_copy(modes_hbm, modes_ref, sems.at[0]),
        pltpu.make_async_copy(extras_hbm, extras_ref, sems.at[1]),
    ]
    for fetch in fetches:
        fetch.start()
    adjoints = (own_ref, next_ref, far_ref, previous_ref)
    directs = [direct_ref.at[n] for n in range(SNAP)]
    here = lax.axis_index("snap")
    transposed = (((1,), (1,)), ((), ()))
    gram = jnp.zeros((M, M), jnp.float32)
    for comp in range(COMPONENTS):
        for t in range(0, TILES, 2):
            gram = gram + lax.dot_general(
                columns(directs, comp, (t, t + 1)),
                columns(adjoints, comp, (t, t + 1)),
                transposed,
                preferred_element_type=jnp.float32,
            )
    for fetch in fetches:
        fetch.wait()
    turned, weight = (
        jnp.concatenate([extras_ref[at], extras_ref[at + 1]], axis=1).astype(jnp.bfloat16)
        for at in (TURNED_AT, WEIGHT_AT)
    )
    edges = jnp.dot(turned, columns(adjoints, COMPONENTS, (0, 1)), preferred_element_type=jnp.float32)
    edges = edges.astype(jnp.bfloat16).astype(jnp.float32)
    below, above = edges[:, :NZ], edges[:, NZ:]
    before = [before_ref[n].astype(jnp.float32) for n in range(6)]
    after = [after_ref[n].astype(jnp.float32) for n in range(6)]
    for comp in range(COMPONENTS):
        for t in range(0, TILES, 2):
            adjoint = columns(adjoints, comp, (t, t + 1))
            modes = jnp.dot(weight, adjoint, preferred_element_type=jnp.float32)
            high = modes.astype(jnp.bfloat16)
            rest = modes - high.astype(jnp.float32)
            middle = rest.astype(jnp.bfloat16)
            low = (rest - middle.astype(jnp.float32)).astype(jnp.bfloat16)
            for part, value in enumerate((high, middle, low)):
                parts_ref[comp, part * R : (part + 1) * R, t * NZ : (t + 2) * NZ] = value
        weighted_terms(comp, modes_ref, extras_ref, before, after, below, above, weighted_ref)
    gram = gram * scale
    gram_ref[0] = gram[:, :NZ]
    gram_ref[1] = gram[:, NZ:]
    for core in range(2):
        for snap in range(SNAP):
            half, at = snap // 2, (snap % 2) * COLS
            halves = [
                gram_ref[half, pl.ds(2 * core + t, M // 4, stride=4), :][:, at : at + COLS]
                for t in range(2)
            ]
            chunk = core * SNAP + lax.rem(here + snap, SNAP)
            out_ref[chunk, :64, :] = jnp.concatenate(halves, axis=1)
    blocks = []
    row = 0
    for target, members in enumerate(MEMBERS):
        count = len(members) * R
        product = lax.dot_general(
            parts_ref[target],
            weighted_ref[row : row + count, :],
            transposed,
            preferred_element_type=jnp.float32,
        )
        row += count
        blocks.append((product[:R] + (product[R : 2 * R] + product[2 * R :])) * scale)
    for snap in range(SNAP):
        own = jnp.concatenate(
            [
                block[:, snap * (block.shape[1] // SNAP) : (snap + 1) * (block.shape[1] // SNAP)]
                for block in blocks
            ],
            axis=1,
        )
        for core in range(2):
            for w in range(4):
                rows = own[(2 * w + core) * 8 : (2 * w + core + 1) * 8]
                out_ref[core * SNAP + snap, 64 + w * 8 : 64 + w * 8 + 8, :] = rows[:, :NZ]
                out_ref[core * SNAP + snap, 96 + w * 8 : 96 + w * 8 + 8, :] = rows[:, NZ:]
    core = lax.axis_index("core")
    keep_ref[...] = out_ref[pl.ds(core * SNAP, SNAP)]
    send_ref[...] = out_ref[pl.ds((1 - core) * SNAP, SNAP)]


def finish_kernel(sums_ref, gram_ref, reduced_ref):
    total = jnp.sum(sums_ref[...], axis=0)
    gram_ref[...] = jnp.concatenate([total[0:1, :COLS], total[0:1, COLS:]], axis=0)
    reduced_ref[...] = jnp.concatenate(
        [total[1:2, v * OWN : (v + 1) * OWN] for v in range(8)], axis=0
    )


def call(kernel, out_shape, flops, moved, scratch=(), inputs=None, outputs=None, limit=LIMIT):
    def run(*operands):
        spaces = dict.fromkeys(range(len(operands)), pltpu.VMEM) | (inputs or {})
        results = pl.BlockSpec(memory_space=outputs or pltpu.VMEM)
        several = isinstance(out_shape, tuple)
        return pl.pallas_call(
            kernel,
            out_shape=out_shape,
            in_specs=[pl.BlockSpec(memory_space=space) for space in spaces.values()],
            out_specs=[results] * len(out_shape) if several else results,
            scratch_shapes=list(scratch),
            compiler_params=pltpu.CompilerParams(vmem_limit_bytes=limit),
            cost_estimate=pl.CostEstimate(flops=flops, bytes_accessed=moved, transcendentals=0),
        )(*operands)

    return run


def shards(direct_snaps, adjoint_snaps, left_factor, right_factor, singular, term_coeff, term_slot):
    scale = 1.0 / math.sqrt(1572864)
    back = -COLS * lax.axis_index("snap")
    left = mode_weight(jnp.roll(left_factor, back, axis=0), singular).T
    right = mode_weight(right_factor, singular).T
    turned = jnp.roll(right, back, axis=1)
    tiles = COMPONENTS * TILES

    def shape(*dims, dtype=jnp.bfloat16):
        return jax.ShapeDtypeStruct(dims, dtype)

    spread_shape = shape(SNAP, tiles, COLS, NZ)
    ready = call(
        direct_kernel,
        pltpu.HBM(spread_shape.shape, jnp.bfloat16),
        0,
        3 << 20,
        (
            pltpu.VMEM(direct_snaps.shape, jnp.bfloat16),
            pltpu.VMEM((SNAP, tiles, COLS, NZ), jnp.bfloat16),
            pltpu.SemaphoreType.DMA((PIECES,)),
            pltpu.SemaphoreType.DMA((PIECES,)),
        ),
        {0: pl.ANY},
        pltpu.HBM,
        WHOLE,
    )(direct_snaps)
    direct = lax.all_to_all(ready, "snap", 0, 0, tiled=True)
    selector = (
        term_slot[jnp.array(ORDER)][None, :] == jnp.arange(TERMS, dtype=jnp.int32)[:, None]
    ).astype(jnp.float32)
    here = lax.axis_index("snap").astype(jnp.int32).reshape(1)
    piece = (SENT, COLS, NZ)
    own, *others, direct_weight = call(
        adjoint_kernel,
        (
            pltpu.HBM(piece, jnp.bfloat16),
            *[shape(*piece)] * (SNAP - 1),
            pltpu.HBM((R, M), jnp.bfloat16),
        ),
        0,
        3 << 20,
        (pltpu.VMEM((SNAP, *piece), jnp.bfloat16),),
        {0: pltpu.SMEM},
    )(here, adjoint_snaps, ready, right)
    arrived = [
        lax.ppermute(piece, "snap", [(i, (i + n) % SNAP) for i in range(SNAP)])
        for n, piece in enumerate(others, 1)
    ]
    adjoints = (own, *arrived[::-1])
    modes, first, last = call(
        modes_kernel,
        (pltpu.HBM((tiles, R, NZ), jnp.float32), shape(6, R, NZ), shape(6, R, NZ)),
        2 * R * M * 3 * CELLS,
        2 << 20,
    )(direct, direct_weight)
    modes = pltpu.with_memory_space_constraint(modes, pltpu.HBM)
    extras, selector = call(
        extras_kernel,
        (pltpu.HBM((EXTRAS, R, NZ), jnp.float32), pltpu.HBM((TERMS, TERMS), jnp.float32)),
        0,
        1 << 20,
        inputs={0: pltpu.SMEM, 5: pltpu.HBM},
    )(here, left, turned, term_coeff, selector, modes)
    extras = pltpu.with_memory_space_constraint(extras, pltpu.HBM)
    slabs = [(i, i + 1) for i in range(127)]
    before = lax.ppermute(last, SPACE, slabs)
    after = lax.ppermute(first, SPACE, [(j, i) for i, j in slabs])
    half = shape(SNAP, 128, NZ, dtype=jnp.float32)
    keep, send = call(
        functools.partial(products_kernel, scale),
        (half, half),
        1 << 30,
        6 << 20,
        (
            pltpu.VMEM(modes.shape, jnp.float32),
            pltpu.VMEM(extras.shape, jnp.float32),
            pltpu.VMEM((2, M, NZ), jnp.float32),
            pltpu.VMEM((COMPONENTS, 3 * R, CELLS), jnp.bfloat16),
            pltpu.VMEM((TERMS * R, CELLS), jnp.bfloat16),
            pltpu.VMEM((2 * SNAP, 128, NZ), jnp.float32),
            pltpu.SemaphoreType.DMA((2,)),
        ),
        {5: pltpu.HBM, 6: pltpu.HBM},
    )(*adjoints, direct, modes, extras, before, after)
    terms = keep + lax.ppermute(send, "core", [(0, 1), (1, 0)])
    near = lax.all_to_all(terms, "snap", 0, 0, tiled=True).sum(axis=0)
    gram = near[:64]
    operators = near[64:].reshape(2, 4, 8, 8, OWN).transpose(0, 3, 1, 2, 4).reshape(TERMS, 4 * NZ)
    ordered = jnp.dot(selector, operators, precision=lax.Precision.HIGHEST)
    owned = jnp.stack([gram, ordered.reshape(64, NZ)], axis=1)
    sums = lax.all_to_all(owned, ("z", "y"), 0, 0, tiled=True)
    outs = (shape(2, COLS, dtype=jnp.float32), shape(8, OWN, dtype=jnp.float32))
    gram, reduced = call(finish_kernel, outs, 0, 1 << 16)(sums)
    return (gram.T, reduced)


def solution(mesh):
    parts = Mesh(mesh.devices.reshape(8, 8, 2, 4), SPACE + ("snap",))
    return jax.shard_map(
        shards,
        mesh=parts,
        in_specs=(
            P("snap", None, SPACE, None, None),
            P("snap", None, SPACE, None, None),
            P(),
            P(),
            P(),
            P(None, SPACE, None, None),
            P(),
        ),
        out_specs=(P("snap", SPACE), P(SPACE, "snap")),
        check_vma=False,
    )
```

```python
import functools
import math

import jax
import jax.numpy as jnp
from jax import lax
from jax.experimental import pallas as pl
from jax.experimental.pallas import tpu as pltpu
from jax.sharding import Mesh, PartitionSpec as P

stencil_kind = (4, 4, 4, 1, 2, 3, 1, 2, 3, 1, 2, 3, 0, 0, 0, 0)
source_comp = (0, 1, 2, 0, 0, 0, 1, 1, 1, 2, 2, 2, 0, 1, 2, 1)
target_comp = (0, 1, 2, 0, 0, 0, 1, 1, 1, 2, 2, 2, 1, 2, 0, 0)
TERMS = len(stencil_kind)
COMPONENTS = 3
MEMBERS = tuple(
    tuple(q for q in range(TERMS) if target_comp[q] == target) for target in range(COMPONENTS)
)
ORDER = tuple(q for members in MEMBERS for q in members)
M = 256
R = 64
NY = 8
NZ = 128
CELLS = NY * NZ
SNAP = 4
COLS = M // SNAP
OWN = R // SNAP
SPACE = ("z", "y", "core")
PIECES = 4
LIMIT = 24 * 1024 * 1024
WHOLE = 60 * 1024 * 1024


def mode_weight(factor, singular):
    return (factor / jnp.sqrt(singular)[None, :]).astype(jnp.bfloat16)


TILES = 8
GROUP = NZ // SNAP
WEIGHT_AT = 0
COEFF_AT = WEIGHT_AT + 2
TURNED_AT = COEFF_AT + 2
EXTRAS = TURNED_AT + 2
SENT = COMPONENTS * TILES + 2


def spread_rows(layer, out_ref, first, at):
    rows = jnp.swapaxes(layer, 0, 1)
    for half in range(2):
        group = [rows[half * 4 + i] for i in range(4)]
        for quarter in range(SNAP):
            lanes = slice(quarter * GROUP, (quarter + 1) * GROUP)
            out_ref[quarter, first + half, at : at + layer.shape[0]] = jnp.concatenate(
                [row[:, lanes] for row in group], axis=1
            )


def direct_kernel(snaps_ref, out_ref, raw, spread, arrived, sent):
    count = COLS // PIECES
    parts = [pl.ds(n * count, count) for n in range(PIECES)]
    arrivals = [
        pltpu.make_async_copy(snaps_ref.at[part], raw.at[part], arrived.at[n])
        for n, part in enumerate(parts)
    ]
    for copy in arrivals:
        copy.start()
    departures = []
    for n, part in enumerate(parts):
        arrivals[n].wait()
        for comp in range(COMPONENTS):
            for x in range(4):
                spread_rows(raw[part, comp, x], spread, comp * TILES + x * 2, n * count)
        departures.append(
            pltpu.make_async_copy(spread.at[:, :, part], out_ref.at[:, :, part], sent.at[n])
        )
        departures[-1].start()
    for copy in departures:
        copy.wait()


def adjoint_kernel(
    snap_ref,
    snaps_ref,
    ready_ref,
    weight_ref,
    own_ref,
    next_ref,
    far_ref,
    previous_ref,
    weight_out,
    spread,
):
    weight_out[...] = weight_ref[...]
    for comp in range(COMPONENTS):
        for x in range(4):
            spread_rows(snaps_ref[:, comp, x], spread, comp * TILES + x * 2, 0)
    place = lax.rem(lax.broadcasted_iota(jnp.int32, (COLS, NZ), 1), GROUP)
    empty = jnp.zeros((COLS, NZ), jnp.bfloat16)
    spread[0, SENT - 2] = empty
    spread[SNAP - 1, SENT - 1] = empty
    for quarter in range(SNAP):
        low = jnp.zeros((COLS, NZ), jnp.float32)
        high = jnp.zeros((COLS, NZ), jnp.float32)
        for index in range(COMPONENTS * TILES):
            wide = ready_ref[quarter, index].astype(jnp.float32)
            if quarter > 0:
                edge = jnp.where(place == 0, wide, 0.0)
                low = low + (pltpu.roll(edge, index, 1) if index else edge)
            if quarter < SNAP - 1:
                edge = jnp.where(place == GROUP - 1, wide, 0.0)
                high = high + pltpu.roll(edge, NZ + index - (GROUP - 1), 1)
        if quarter > 0:
            spread[quarter - 1, SENT - 1] = low.astype(jnp.bfloat16)
        if quarter < SNAP - 1:
            spread[quarter + 1, SENT - 2] = high.astype(jnp.bfloat16)
    for n, ref in enumerate((own_ref, next_ref, far_ref, previous_ref)):
        ref[...] = spread[lax.rem(snap_ref[0] + n, SNAP)]


def extras_kernel(snap_ref, left_ref, turned_ref, coeff_ref, selector_ref, _, out_ref, selector_out):
    selector_out[...] = selector_ref[...]
    for n in range(2):
        half = slice(n * NZ, (n + 1) * NZ)
        out_ref[WEIGHT_AT + n] = left_ref[:, half].astype(jnp.float32)
        out_ref[TURNED_AT + n] = turned_ref[:, half].astype(jnp.float32)
    shift = lax.rem(NZ - GROUP * snap_ref[0], NZ)
    for q in range(TERMS):
        for x in range(4):
            own = pltpu.roll(coeff_ref[q, x], shift, 1)
            for half in range(2):
                row = q * TILES + x * 2 + half
                out_ref[COEFF_AT + row // R, row % R : row % R + 1, :] = jnp.concatenate(
                    [own[half * 4 + i : half * 4 + i + 1, :GROUP] for i in range(4)], axis=1
                )


def columns(refs, comp, tiles):
    return jnp.concatenate(
        [
            jnp.concatenate([ref[comp * TILES + t] for ref in refs], axis=0)
            for t in tiles
        ],
        axis=1,
    )


def modes_kernel(snaps_ref, weight_ref, out_ref, first_ref, last_ref):
    weight = weight_ref[...]
    blocks = [snaps_ref.at[n] for n in range(SNAP)]
    for comp in range(COMPONENTS):
        for t in range(0, TILES, 2):
            block = columns(blocks, comp, (t, t + 1))
            modes = jnp.dot(weight, block, preferred_element_type=jnp.float32)
            modes = modes.astype(jnp.bfloat16)
            for half in range(2):
                tile = modes[:, half * NZ : (half + 1) * NZ]
                out_ref[comp * TILES + t + half] = tile.astype(jnp.float32)
                if t == 0:
                    first_ref[comp * 2 + half] = tile
                if t == TILES - 2:
                    last_ref[comp * 2 + half] = tile


def weighted_terms(comp, modes_ref, extras_ref, before, after, below, above, out_ref):
    lane = lax.broadcasted_iota(jnp.int32, (R, NZ), 1)
    place = lax.rem(lane, GROUP)
    base = [0]
    for members in MEMBERS:
        base.append(base[-1] + len(members) * R)

    def put(q, t, value):
        target = target_comp[q]
        count = len(MEMBERS[target])
        at = MEMBERS[target].index(q)
        row = (q * TILES + t) % R
        coeff = extras_ref[COEFF_AT + q * TILES // R, row : row + 1, :]
        value = (value * coeff).astype(jnp.bfloat16)
        for block in range(SNAP):
            row = base[target] + (block * count + at) * OWN
            out_ref[row : row + OWN, t * NZ : (t + 1) * NZ] = value[block * OWN : (block + 1) * OWN]

    field = [modes_ref[comp * TILES + t] for t in range(TILES)]
    down = before[comp * 2 : comp * 2 + 2] + field[:-2]
    up = field[2:] + after[comp * 2 : comp * 2 + 2]
    for x in range(4):
        pair = field[2 * x : 2 * x + 2]
        ahead = [pltpu.roll(v, NZ - GROUP, 1) for v in pair]
        behind = [pltpu.roll(v, GROUP, 1) for v in pair]
        for half in range(2):
            t = 2 * x + half
            index = comp * TILES + t
            center = pair[half]
            x_up, x_down = up[t], down[t]
            y_up = jnp.where(lane >= NZ - GROUP, ahead[1] if half == 0 else 0.0, ahead[half])
            y_down = jnp.where(lane < GROUP, behind[0] if half == 1 else 0.0, behind[half])
            z_up = jnp.where(
                place == GROUP - 1,
                pltpu.roll(above, GROUP - 1 - index, 1),
                pltpu.roll(center, NZ - 1, 1),
            )
            z_down = jnp.where(
                place == 0,
                pltpu.roll(below, NZ - index, 1) if index else below,
                pltpu.roll(center, 1, 1),
            )
            for q in range(TERMS):
                if source_comp[q] != comp:
                    continue
                kind = stencil_kind[q]
                if kind == 0:
                    value = center
                elif kind == 1:
                    value = 0.5 * (x_up - x_down)
                elif kind == 2:
                    value = 0.5 * (y_up - y_down)
                elif kind == 3:
                    value = 0.5 * (z_up - z_down)
                else:
                    beside = x_up + x_down
                    beside = beside + y_up + y_down
                    beside = beside + z_up + z_down
                    value = beside - 6.0 * center
                put(q, t, value)


def products_kernel(
    scale,
    far_ref,
    own_ref,
    next_ref,
    previous_ref,
    direct_ref,
    modes_hbm,
    extras_hbm,
    before_ref,
    after_ref,
    keep_ref,
    send_ref,
    modes_ref,
    extras_ref,
    gram_ref,
    parts_ref,
    weighted_ref,
    out_ref,
    sems,
):
    fetches = [
        pltpu.make_async_copy(modes_hbm, modes_ref, sems.at[0]),
        pltpu.make_async_copy(extras_hbm, extras_ref, sems.at[1]),
    ]
    for fetch in fetches:
        fetch.start()
    adjoints = (own_ref, next_ref, far_ref, previous_ref)
    directs = [direct_ref.at[n] for n in range(SNAP)]
    here = lax.axis_index("snap")
    transposed = (((1,), (1,)), ((), ()))
    gram = jnp.zeros((M, M), jnp.float32)
    for comp in range(COMPONENTS):
        for t in range(0, TILES, 2):
            gram = gram + lax.dot_general(
                columns(directs, comp, (t, t + 1)),
                columns(adjoints, comp, (t, t + 1)),
                transposed,
                preferred_element_type=jnp.float32,
            )
    for fetch in fetches:
        fetch.wait()
    turned, weight = (
        jnp.concatenate([extras_ref[at], extras_ref[at + 1]], axis=1).astype(jnp.bfloat16)
        for at in (TURNED_AT, WEIGHT_AT)
    )
    edges = jnp.dot(turned, columns(adjoints, COMPONENTS, (0, 1)), preferred_element_type=jnp.float32)
    edges = edges.astype(jnp.bfloat16).astype(jnp.float32)
    below, above = edges[:, :NZ], edges[:, NZ:]
    before = [before_ref[n].astype(jnp.float32) for n in range(6)]
    after = [after_ref[n].astype(jnp.float32) for n in range(6)]
    for comp in range(COMPONENTS):
        for t in range(0, TILES, 2):
            adjoint = columns(adjoints, comp, (t, t + 1))
            modes = jnp.dot(weight, adjoint, preferred_element_type=jnp.float32)
            high = modes.astype(jnp.bfloat16)
            rest = modes - high.astype(jnp.float32)
            middle = rest.astype(jnp.bfloat16)
            low = (rest - middle.astype(jnp.float32)).astype(jnp.bfloat16)
            for part, value in enumerate((high, middle, low)):
                parts_ref[comp, part * R : (part + 1) * R, t * NZ : (t + 2) * NZ] = value
        weighted_terms(comp, modes_ref, extras_ref, before, after, below, above, weighted_ref)
    gram = gram * scale
    gram_ref[0] = gram[:, :NZ]
    gram_ref[1] = gram[:, NZ:]
    for core in range(2):
        for snap in range(SNAP):
            half, at = snap // 2, (snap % 2) * COLS
            halves = [
                gram_ref[half, pl.ds(2 * core + t, M // 4, stride=4), :][:, at : at + COLS]
                for t in range(2)
            ]
            chunk = core * SNAP + lax.rem(here + snap, SNAP)
            out_ref[chunk, :64, :] = jnp.concatenate(halves, axis=1)
    blocks = []
    row = 0
    for target, members in enumerate(MEMBERS):
        count = len(members) * R
        product = lax.dot_general(
            parts_ref[target],
            weighted_ref[row : row + count, :],
            transposed,
            preferred_element_type=jnp.float32,
        )
        row += count
        blocks.append((product[:R] + (product[R : 2 * R] + product[2 * R :])) * scale)
    for snap in range(SNAP):
        own = jnp.concatenate(
            [
                block[:, snap * (block.shape[1] // SNAP) : (snap + 1) * (block.shape[1] // SNAP)]
                for block in blocks
            ],
            axis=1,
        )
        for core in range(2):
            for w in range(4):
                rows = own[(2 * w + core) * 8 : (2 * w + core + 1) * 8]
                out_ref[core * SNAP + snap, 64 + w * 8 : 64 + w * 8 + 8, :] = rows[:, :NZ]
                out_ref[core * SNAP + snap, 96 + w * 8 : 96 + w * 8 + 8, :] = rows[:, NZ:]
    core = lax.axis_index("core")
    keep_ref[...] = out_ref[pl.ds(core * SNAP, SNAP)]
    send_ref[...] = out_ref[pl.ds((1 - core) * SNAP, SNAP)]


def finish_kernel(sums_ref, gram_ref, reduced_ref):
    total = jnp.sum(sums_ref[...], axis=0)
    gram_ref[...] = jnp.concatenate([total[0:1, :COLS], total[0:1, COLS:]], axis=0)
    reduced_ref[...] = jnp.concatenate(
        [total[1:2, v * OWN : (v + 1) * OWN] for v in range(8)], axis=0
    )


def call(kernel, out_shape, flops, moved, scratch=(), inputs=None, outputs=None, limit=LIMIT):
    def run(*operands):
        spaces = dict.fromkeys(range(len(operands)), pltpu.VMEM) | (inputs or {})
        results = pl.BlockSpec(memory_space=outputs or pltpu.VMEM)
        several = isinstance(out_shape, tuple)
        return pl.pallas_call(
            kernel,
            out_shape=out_shape,
            in_specs=[pl.BlockSpec(memory_space=space) for space in spaces.values()],
            out_specs=[results] * len(out_shape) if several else results,
            scratch_shapes=list(scratch),
            compiler_params=pltpu.CompilerParams(vmem_limit_bytes=limit),
            cost_estimate=pl.CostEstimate(flops=flops, bytes_accessed=moved, transcendentals=0),
        )(*operands)

    return run


def shards(direct_snaps, adjoint_snaps, left_factor, right_factor, singular, term_coeff, term_slot):
    scale = 1.0 / math.sqrt(1572864)
    back = -COLS * lax.axis_index("snap")
    left = mode_weight(jnp.roll(left_factor, back, axis=0), singular).T
    right = mode_weight(right_factor, singular).T
    turned = jnp.roll(right, back, axis=1)
    tiles = COMPONENTS * TILES

    def shape(*dims, dtype=jnp.bfloat16):
        return jax.ShapeDtypeStruct(dims, dtype)

    spread_shape = shape(SNAP, tiles, COLS, NZ)
    ready = call(
        direct_kernel,
        pltpu.HBM(spread_shape.shape, jnp.bfloat16),
        0,
        3 << 20,
        (
            pltpu.VMEM(direct_snaps.shape, jnp.bfloat16),
            pltpu.VMEM((SNAP, tiles, COLS, NZ), jnp.bfloat16),
            pltpu.SemaphoreType.DMA((PIECES,)),
            pltpu.SemaphoreType.DMA((PIECES,)),
        ),
        {0: pl.ANY},
        pltpu.HBM,
        WHOLE,
    )(direct_snaps)
    direct = lax.all_to_all(ready, "snap", 0, 0, tiled=True)
    selector = (
        term_slot[jnp.array(ORDER)][None, :] == jnp.arange(TERMS, dtype=jnp.int32)[:, None]
    ).astype(jnp.float32)
    here = lax.axis_index("snap").astype(jnp.int32).reshape(1)
    piece = (SENT, COLS, NZ)
    own, *others, direct_weight = call(
        adjoint_kernel,
        (
            pltpu.HBM(piece, jnp.bfloat16),
            *[shape(*piece)] * (SNAP - 1),
            pltpu.HBM((R, M), jnp.bfloat16),
        ),
        0,
        3 << 20,
        (pltpu.VMEM((SNAP, *piece), jnp.bfloat16),),
        {0: pltpu.SMEM},
    )(here, adjoint_snaps, ready, right)
    arrived = [
        lax.ppermute(piece, "snap", [(i, (i + n) % SNAP) for i in range(SNAP)])
        for n, piece in enumerate(others, 1)
    ]
    previous, far, following = arrived
    adjoints = (far, own, following, previous)
    modes, first, last = call(
        modes_kernel,
        (pltpu.HBM((tiles, R, NZ), jnp.float32), shape(6, R, NZ), shape(6, R, NZ)),
        2 * R * M * 3 * CELLS,
        2 << 20,
    )(direct, direct_weight)
    modes = pltpu.with_memory_space_constraint(modes, pltpu.HBM)
    extras, selector = call(
        extras_kernel,
        (pltpu.HBM((EXTRAS, R, NZ), jnp.float32), pltpu.HBM((TERMS, TERMS), jnp.float32)),
        0,
        1 << 20,
        inputs={0: pltpu.SMEM, 5: pltpu.HBM},
    )(here, left, turned, term_coeff, selector, modes)
    extras = pltpu.with_memory_space_constraint(extras, pltpu.HBM)
    slabs = [(i, i + 1) for i in range(127)]
    before = lax.ppermute(last, SPACE, slabs)
    after = lax.ppermute(first, SPACE, [(j, i) for i, j in slabs])
    half = shape(SNAP, 128, NZ, dtype=jnp.float32)
    keep, send = call(
        functools.partial(products_kernel, scale),
        (half, half),
        1 << 30,
        6 << 20,
        (
            pltpu.VMEM(modes.shape, jnp.float32),
            pltpu.VMEM(extras.shape, jnp.float32),
            pltpu.VMEM((2, M, NZ), jnp.float32),
            pltpu.VMEM((COMPONENTS, 3 * R, CELLS), jnp.bfloat16),
            pltpu.VMEM((TERMS * R, CELLS), jnp.bfloat16),
            pltpu.VMEM((2 * SNAP, 128, NZ), jnp.float32),
            pltpu.SemaphoreType.DMA((2,)),
        ),
        {5: pltpu.HBM, 6: pltpu.HBM},
    )(*adjoints, direct, modes, extras, before, after)
    terms = keep + lax.ppermute(send, "core", [(0, 1), (1, 0)])
    near = lax.all_to_all(terms, "snap", 0, 0, tiled=True).sum(axis=0)
    gram = near[:64]
    operators = near[64:].reshape(2, 4, 8, 8, OWN).transpose(0, 3, 1, 2, 4).reshape(TERMS, 4 * NZ)
    ordered = jnp.dot(selector, operators, precision=lax.Precision.HIGHEST)
    owned = jnp.stack([gram, ordered.reshape(64, NZ)], axis=1)
    sums = lax.all_to_all(owned, ("z", "y"), 0, 0, tiled=True)
    outs = (shape(2, COLS, dtype=jnp.float32), shape(8, OWN, dtype=jnp.float32))
    gram, reduced = call(finish_kernel, outs, 0, 1 << 16)(sums)
    return (gram.T, reduced)


def solution(mesh):
    parts = Mesh(mesh.devices.reshape(8, 8, 2, 4), SPACE + ("snap",))
    return jax.shard_map(
        shards,
        mesh=parts,
        in_specs=(
            P("snap", None, SPACE, None, None),
            P("snap", None, SPACE, None, None),
            P(),
            P(),
            P(),
            P(None, SPACE, None, None),
            P(),
        ),
        out_specs=(P("snap", SPACE), P(SPACE, "snap")),
        check_vma=False,
    )
```
